256 devices in a mesh: atm: 32 (over z, y_hi, core), ocn: 8 (over x, y_lo).
Axes of the slice: x: 4, y: 4 (y_hi: 2, y_lo: 2; y = y_hi * 2 + y_lo), z: 8, core: 2. Of those that a mesh axis runs over, the one named last changes fastest.
Arguments:
- atm_state: float32 [7, 72, 128, 512], P(None, 'ocn', 'atm'), may hold values from -6 to 6
- level_diffusion: float32 [72], P('ocn'), may hold values from 0.05 to 0.2
- level_wind: float32 [72], P('ocn'), may hold values from -0.2 to 0.2
- vertical_rate: float32 [7], replicated, may hold values from 0.05 to 0.2
- convective_rate: float32 [7], replicated, may hold values from 0.05 to 0.4
- ocean_skin: float32 [65536], P(('atm', 'ocn')), may hold values from -6 to 6
- trigger: int32 [65536], P(('atm', 'ocn')), may hold values from 0 to 1, as said below
- group_order: int32 [65536], P(('atm', 'ocn')), may hold values from 0 to 255, as said below
- ocean_state: float32 [2, 20, 262144], P(None, None, ('atm', 'ocn')), may hold values from -6 to 6
- ocean_neighbors: int32 [6, 262144], P(None, ('atm', 'ocn')), may hold values from -32 to 32, as said below
- flux_sources: int32 [4, 262144], P(None, ('atm', 'ocn')), may hold values from 0 to 65535, as said below
- flux_weights: float32 [4, 262144], P(None, ('atm', 'ocn')), may hold values from 0.1 to 0.5
- surface_sources: int32 [4, 65536], P(None, ('atm', 'ocn')), may hold values from 0 to 262143, as said below
- surface_weights: float32 [4, 65536], P(None, ('atm', 'ocn')), may hold values from 0.1 to 0.5
Outputs:
- atm_new: float32 [7, 72, 128, 512], P(None, 'ocn', 'atm')
- ocean_new: float32 [2, 20, 262144], P(None, None, ('atm', 'ocn'))
- surface_new: float32 [65536], P(('atm', 'ocn'))
The draws below stay inside these ranges and needn't reach their ends.
Inputs may be any that keep to these rules, and one draw needn't show every extreme that they name: `group_order`: within each block of 256 entries the values are a permutation of 0 to 255. `trigger`: every aligned run of 8 entries holds equally many ones within a block of 256, so each physics group (run k of every device of an ocn index) holds exactly 64 ones. One block of 256 holds at most 160 ones, and some block holds exactly that many. `ocean_neighbors`: cell plus offset is always a cell of the grid. `flux_sources`: the sources of cell c lie within 8 columns of c // 4. `surface_sources`: the sources of column k lie within 32 cells of 4 * k.
All inputs are finite; a program needn't handle non-finite values.
Results may differ from the reference program's by a relative error of at most 0.00007.
Values sent between devices are 32-bit elements; how exact they have to be, the bound alone decides.
A program may use at most 64 MiB of HBM per device.

```python
import math
import jax
import jax.numpy as jnp

FIELDS = 7
LEV = 72
LON = 512
DYN_STEPS = 4
PHYS_ITERS = 3
CONV_ITERS = 24
OLEV = 20
RATIO = 4
NBR = 6
NW = 4
HW = 32
RW = 8
RW2 = 32
OSTEPS = 4
ROWS = 128
COLS = 65536
PC = 256
SLOT = 8
OCELLS = 262144
N_ATM = 32
N_OCN = 8


def draw_trigger(key, part):
    key = jax.random.fold_in(key, 5)
    blocks = N_ATM * N_OCN
    atm_index = jnp.arange(blocks) // N_OCN
    tropical = (atm_index >= N_ATM * 3 // 8) & (atm_index < N_ATM * 5 // 8)
    hot_runs = jnp.where(tropical, SLOT * 5 // 8, SLOT // 8)
    scores = jax.random.randint(key, (blocks, PC // SLOT, SLOT), 0, 1 << 20) * SLOT + jnp.arange(SLOT)[None, None, :]
    rank = jnp.argsort(jnp.argsort(scores, axis=-1), axis=-1)
    marks = (rank < hot_runs[:, None, None]).astype(jnp.int32)
    return marks.reshape(-1)


def draw_group_order(key, part):
    key = jax.random.fold_in(key, 7)
    blocks = N_ATM * N_OCN
    device_keys = jax.random.split(key, blocks)
    orders = jax.vmap(lambda k: jax.random.permutation(k, PC).astype(jnp.int32))(device_keys)
    return orders.reshape(-1).astype(jnp.int32)


def reach_draw(key, centre, reach, shape, limit):
    sign_key, size_key = jax.random.split(key)
    signs = jnp.where(jax.random.bernoulli(sign_key, 0.5, shape), 1, -1)
    sizes = jax.random.randint(size_key, shape, 1, reach + 1)
    sizes = sizes.at[0].set(reach)
    return jnp.clip(centre[None, :] + signs * sizes, 0, limit - 1).astype(jnp.int32)


def draw_ocean_neighbors(key, part):
    key = jax.random.fold_in(key, 11)
    centre = jnp.arange(OCELLS, dtype=jnp.int32)
    target = reach_draw(key, centre, HW, (NBR, OCELLS), OCELLS)
    return (target - centre[None, :]).astype(jnp.int32)


def draw_flux_sources(key, part):
    key = jax.random.fold_in(key, 23)
    return reach_draw(key, jnp.arange(OCELLS) // RATIO, RW, (NW, OCELLS), COLS)


def draw_surface_sources(key, part):
    key = jax.random.fold_in(key, 37)
    return reach_draw(key, jnp.arange(COLS) * RATIO, RW2, (NW, COLS), OCELLS)


def level_of(key, shape, cuts, smallest, top_value):
    level = 1.0
    for position, blocks in cuts:
        steps = jax.random.uniform(jax.random.fold_in(jax.random.fold_in(key, 6), position), (blocks,), jnp.float32, smallest / len(cuts), top_value / len(cuts))
        level = level * jnp.repeat(jnp.exp(steps), shape[position] // blocks).reshape((-1,) + (1,) * (len(shape) - 1 - position))
    return level


def noise(key, dims, width, most, cuts=(), held_as=jnp.bfloat16):
    values = width * jax.random.normal(key, dims, jnp.float32)
    if cuts:
        values = values * level_of(key, dims, cuts, -0.22, 0.18)
    return jnp.clip(values, -most, most).astype(held_as)


def setup_inputs(seed: int = 0) -> dict:
    keys = jax.random.split(jax.random.key(seed), 15)
    return {
        "atm_state": noise(keys[0], (FIELDS, LEV, ROWS, LON), 1.0, 6.0, ((1, 8), (2, 32)), jnp.float32),
        "level_diffusion": jnp.clip(0.05 + 0.15 * jax.random.uniform(keys[1], (LEV,), jnp.float32) ** level_of(keys[1], (LEV,), ((0, 8),), -0.2, 0.2), 0.05, 0.2),
        "level_wind": jnp.clip(jax.random.uniform(keys[2], (LEV,), jnp.float32, -0.2, 0.2) * level_of(keys[2], (LEV,), ((0, 8),), -0.4, 0.0), -0.2, 0.2),
        "vertical_rate": jnp.clip(jnp.exp(jax.random.uniform(keys[3], (FIELDS,), jnp.float32, math.log(0.05), math.log(0.2))), 0.05, 0.2),
        "convective_rate": jnp.clip(jnp.exp(jax.random.uniform(keys[4], (FIELDS,), jnp.float32, math.log(0.05), math.log(0.4))), 0.05, 0.4),
        "ocean_skin": noise(keys[5], (COLS,), 1.0, 6.0, ((0, 256),), jnp.float32),
        "trigger": draw_trigger(jax.random.fold_in(keys[14], 71), 0),
        "group_order": draw_group_order(jax.random.fold_in(keys[14], 71), 0),
        "ocean_state": noise(keys[8], (2, OLEV, OCELLS), 1.0, 6.0, ((2, 256),), jnp.float32),
        "ocean_neighbors": draw_ocean_neighbors(jax.random.fold_in(keys[14], 71), 0),
        "flux_sources": draw_flux_sources(jax.random.fold_in(keys[14], 71), 0),
        "flux_weights": jnp.clip(0.1 + 0.4 * jax.random.uniform(keys[11], (NW, OCELLS), jnp.float32) ** level_of(keys[11], (NW, OCELLS), ((1, 256),), -0.2, 0.2), 0.1, 0.5),
        "surface_sources": draw_surface_sources(jax.random.fold_in(keys[14], 71), 0),
        "surface_weights": jnp.clip(0.1 + 0.4 * jax.random.uniform(keys[13], (NW, COLS), jnp.float32) ** level_of(keys[13], (NW, COLS), ((1, 256),), -0.2, 0.2), 0.1, 0.5),
    }


OCEAN_SPREAD = 0.6
OCEAN_VERTICAL = 0.2
HEAT_COEF = 0.5
MOIST_COEF = 0.5
HEAT_BACK = 0.3
MOIST_BACK = 0.3
OCEAN_FORCE = 0.3

def grid_step(prognostic, padded, level_diffusion, level_wind):
    northern = padded[:, :, :-2]
    southern = padded[:, :, 2:]
    eastern = jnp.roll(prognostic, -1, axis=3)
    western = jnp.roll(prognostic, 1, axis=3)
    laplace = northern + southern + eastern + western - 4.0 * prognostic
    return prognostic + level_diffusion[None, :, None, None] * laplace - level_wind[None, :, None, None] * 0.5 * (eastern - western)

def vertical(columns, vertical_rate):
    for repeat in range(PHYS_ITERS):
        padded = jnp.concatenate([columns[:, :1], columns, columns[:, -1:]], axis=1)
        columns = columns + vertical_rate[:, None, None] * (padded[:, 2:] + padded[:, :-2] - 2.0 * columns)
    return columns

def convect(columns, convective_rate, trigger_mask):
    for repeat in range(CONV_ITERS):
        transfer = convective_rate[:, None, None] * jnp.tanh(columns[:, 1:] - columns[:, :-1]) * trigger_mask
        columns = columns + jnp.pad(transfer, ((0, 0), (0, 1), (0, 0))) - jnp.pad(transfer, ((0, 0), (1, 0), (0, 0)))
    return columns

def surface(columns, skin_value):
    lowest = columns[:, -1, :]
    wind_speed = jnp.sqrt(1.0 + lowest[1] * lowest[1] + lowest[2] * lowest[2])
    heat_flux = HEAT_COEF * wind_speed * (lowest[0] - skin_value)
    fresh_flux = MOIST_COEF * wind_speed * lowest[3]
    columns = columns.at[0, -1].add(-HEAT_BACK * heat_flux)
    columns = columns.at[3, -1].add(-MOIST_BACK * fresh_flux)
    return (columns, jnp.stack([heat_flux, fresh_flux]))

def ocean_update(ocean_fields, beside_all, forcing):
    blended = ocean_fields + OCEAN_SPREAD * (beside_all / 6.0 - ocean_fields)
    padded = jnp.concatenate([blended[:, :1], blended, blended[:, -1:]], axis=1)
    blended = blended + OCEAN_VERTICAL * (padded[:, 2:] + padded[:, :-2] - 2.0 * blended)
    return blended.at[:, 0].add(OCEAN_FORCE * forcing)

def place_active(order_block, trigger_block):
    return jnp.zeros(order_block.shape, jnp.int32).at[order_block].set(trigger_block)

def reference(atm_state, level_diffusion, level_wind, vertical_rate, convective_rate, ocean_skin, trigger, group_order, ocean_state, ocean_neighbors, flux_sources, flux_weights, surface_sources, surface_weights):
    prognostic = atm_state
    for repeat in range(DYN_STEPS):
        padded = jnp.pad(prognostic, ((0, 0), (0, 0), (1, 1), (0, 0)))
        prognostic = grid_step(prognostic, padded, level_diffusion, level_wind)
    columns = prognostic.reshape(FIELDS, LEV, COLS)
    columns = vertical(columns, vertical_rate)
    blocks = COLS // PC
    active = jax.vmap(place_active)(group_order.reshape(blocks, PC).astype(jnp.int32), trigger.reshape(blocks, PC).astype(jnp.int32)).reshape(COLS)
    columns = convect(columns, convective_rate, active.astype(jnp.float32)[None, None, :])
    columns, fluxes = surface(columns, ocean_skin)
    atm_new = columns.reshape(FIELDS, LEV, ROWS, LON)
    forcing = jnp.zeros((2, OCELLS), jnp.float32)
    for link in range(NW):
        forcing = forcing + flux_weights[link][None, :] * fluxes[:, flux_sources[link]]
    cell_ids = jnp.arange(OCELLS, dtype=jnp.int32)
    ocean_fields = ocean_state
    for repeat in range(OSTEPS):
        beside_all = jnp.zeros_like(ocean_fields)
        for link in range(NBR):
            beside_all = beside_all + ocean_fields[:, :, cell_ids + ocean_neighbors[link].astype(jnp.int32)]
        ocean_fields = ocean_update(ocean_fields, beside_all, forcing)
    uppermost = ocean_fields[0, 0]
    surface_new = jnp.zeros((COLS,), jnp.float32)
    for link in range(NW):
        surface_new = surface_new + surface_weights[link] * uppermost[surface_sources[link]]
    return (atm_new, ocean_fields, surface_new)
```

```python
import functools

import jax
import jax.numpy as jnp
from jax import lax
from jax.experimental import pallas as pl
from jax.experimental.pallas import tpu as pltpu
from jax.sharding import PartitionSpec as P

MESH = pl.DeviceIdType.MESH
F32 = jnp.float32
BF16 = jnp.bfloat16

FIELDS = 7
LEV = 72
NLEV = 9
ROWS = 4
QS = 4
DYN_STEPS = 4
PHYS_ITERS = 3
CONV_ITERS = 24
OLEV = 20
OSTEPS = 4
NBR = 6
NW = 4
PARTS = 3
OROW = 48
NT = 12
OCEAN_SPREAD = 0.6
OCEAN_VERTICAL = 0.2
HEAT_COEF = 0.5
MOIST_COEF = 0.5
HEAT_BACK = 0.3
MOIST_BACK = 0.3
OCEAN_FORCE = 0.3

GROUPS = ((0, 4), (4, 3))
HSUB = 16


def iota(shape, dim):
    return lax.broadcasted_iota(jnp.int32, shape, dim)


def kernel(
    n_atm,
    n_ocn,
    atm, ld, lw, vr, cr, skin, trig, order, ocean, nbr, fsrc, fw, ssrc, sw,
    out_atm, out_ocean, out_surf,
    ld_s, lw_s, vr_s, cr_s, skin_v, trig_v, order_v, ssrc_v, sw_v,
    nb, d0, d1, coef,
    sa0, ra0, pa0, ba0, sa1, ra1, pa1, ba1,
    xa, xb, out_v,
    oc_l, oc_o, oc_r, nbr_e, fsrc_e, fw_e,
    st, hs, mm, ff, uu, oout, sout,
    fl, fl_l, fl_r,
    local_sem, halo_send, halo_recv, oh_send, oh_recv,
    a_send, a_recv, b_send, b_recv, self_sem, f_send, f_recv, out_sem,
):
    a = lax.axis_index("atm")
    o = lax.axis_index("ocn")
    dev = a * n_ocn + o
    up = lax.rem(a + n_atm - 1, n_atm)
    down = lax.rem(a + 1, n_atm)
    total = n_atm * n_ocn
    left = lax.rem(dev + total - 1, total)
    right = lax.rem(dev + 1, total)
    left_id = (left // n_ocn, lax.rem(left, n_ocn))
    right_id = (right // n_ocn, lax.rem(right, n_ocn))
    peers = [lax.rem(o + d, n_ocn) for d in range(1, n_ocn)]

    fills = [
        (ld, ld_s), (lw, lw_s), (vr, vr_s), (cr, cr_s),
        (skin, skin_v), (trig, trig_v), (order, order_v), (ssrc, ssrc_v), (sw, sw_v),
        (atm, nb.at[1]), (ocean, oc_o),
        (nbr, nbr_e.at[:, pl.ds(256, 1024)]),
        (fsrc, fsrc_e.at[:, pl.ds(256, 1024)]),
        (fw, fw_e.at[:, pl.ds(256, 1024)]),
    ]
    fills = [
        pltpu.make_async_copy(src, dst, local_sem.at[i]) for i, (src, dst) in enumerate(fills)
    ]
    for copy in fills:
        copy.start()

    barrier = pltpu.get_barrier_semaphore()
    partners = [(up, o), (down, o), left_id, right_id] + [(a, p) for p in peers]
    for partner in partners:
        pl.semaphore_signal(barrier, inc=1, device_id=partner, device_id_type=MESH)
    pl.semaphore_wait(barrier, len(partners))

    def remote(src, dst, send, recv, device):
        return pltpu.make_async_remote_copy(
            src_ref=src, dst_ref=dst, send_sem=send, recv_sem=recv,
            device_id=device, device_id_type=MESH,
        )

    def halo(g):
        f0, nf = GROUPS[g]
        rows = pl.ds(f0 * NLEV * HSUB, nf * NLEV * HSUB)
        return [
            remote(atm.at[rows], nb.at[0, rows], halo_send.at[g, 0], halo_recv.at[g, 0], (down, o)),
            remote(atm.at[rows], nb.at[2, rows], halo_send.at[g, 1], halo_recv.at[g, 1], (up, o)),
        ]

    halos = [halo(0), halo(1)]
    for copy in halos[0]:
        copy.start()

    ocean3 = ocean.reshape(OLEV, 16, 128)
    last, first = pl.ds(768, 256), pl.ds(0, 256)
    low, high = pl.ds(0, 256), pl.ds(1280, 256)
    edge = [
        (ocean3.at[:, pl.ds(8, 8)], oc_l.reshape(OLEV, 8, 128), right_id),
        (nbr.at[:, last], nbr_e.at[:, low], right_id),
        (fsrc.at[:, last], fsrc_e.at[:, low], right_id),
        (fw.at[:, last], fw_e.at[:, low], right_id),
        (ocean3.at[:, pl.ds(0, 8)], oc_r.reshape(OLEV, 8, 128), left_id),
        (nbr.at[:, first], nbr_e.at[:, high], left_id),
        (fsrc.at[:, first], fsrc_e.at[:, high], left_id),
        (fw.at[:, first], fw_e.at[:, high], left_id),
    ]
    edges = [
        remote(src, dst, oh_send.at[i], oh_recv.at[i], device)
        for i, (src, dst, device) in enumerate(edge)
    ]
    for copy in edges:
        copy.start()
    for copy in halos[1]:
        copy.start()

    for copy in fills:
        copy.wait()

    hit = jnp.where(trig_v[...] > 0, order_v[...], -1).astype(F32)
    hit = jnp.concatenate([hit, jnp.full((6, 128), -1.0, F32)], axis=0)
    hit = jnp.transpose(hit, (1, 0))
    lane = iota((128, 128), 1)
    active = []
    for half in range(2):
        column = (lane + 128 * half).astype(F32)
        mark = jnp.where(hit[:, 0:1] == column, 1.0, 0.0) + jnp.where(hit[:, 1:2] == column, 1.0, 0.0)
        active.append(jnp.sum(mark, axis=0, keepdims=True))

    for copy in edges:
        copy.wait_recv()

    unused = jnp.zeros((4, 128), F32)
    for u in range(NT):
        for f in range(2):
            if u < 2:
                piece = oc_l[pl.ds((u + 2) * 2 + f, OLEV, stride=8), :]
            elif u < 10:
                piece = oc_o[pl.ds((u - 2) * 2 + f, OLEV, stride=16), :]
            else:
                piece = oc_r[pl.ds((u - 10) * 2 + f, OLEV, stride=8), :]
            st[pl.ds(u * OROW + f * 24, OLEV), :] = piece
            st[pl.ds(u * OROW + f * 24 + OLEV, 4), :] = unused

    def build(u, carry):
        at = pl.multiple_of(u * 128, 128)
        k = iota((192, 128), 0) + 96
        base = iota((1, 128), 1) + 128
        count = jnp.zeros((192, 128), F32)
        for j in range(NBR):
            target = nbr_e[pl.ds(j, 1), pl.ds(at, 128)] + base
            count = count + jnp.where(k == target, 1.0, 0.0)
        mm[u - 1, pl.ds(0, 96), :] = jnp.zeros((96, 128), BF16)
        mm[u - 1, pl.ds(96, 192), :] = count.astype(BF16)
        mm[u - 1, pl.ds(288, 96), :] = jnp.zeros((96, 128), BF16)
        return carry

    lax.fori_loop(1, NT - 1, build, 0)

    level_row = lax.rem(iota((OROW, 128), 0), 24)

    def spread(force):
        def split(u, carry):
            rest = st[pl.ds(pl.multiple_of(u * OROW, OROW), OROW), :]
            for part in range(PARTS):
                piece = rest.astype(BF16)
                hs[u, pl.ds(part * OROW, OROW), :] = piece
                rest = rest - piece.astype(F32)
            return carry

        lax.fori_loop(0, NT, split, 0)

        def tile(u, carry):
            source = jnp.concatenate([hs[u - 1], hs[u], hs[u + 1]], axis=1)
            sums = jnp.dot(source, mm[u - 1], preferred_element_type=F32)
            around = sums[0:OROW]
            for part in range(1, PARTS):
                around = around + sums[part * OROW : (part + 1) * OROW]
            rows = pl.ds(pl.multiple_of(u * OROW, OROW), OROW)
            here = st[rows, :]
            here = here + OCEAN_SPREAD * (around * (1.0 / 6.0) - here)
            above = jnp.where(level_row == 0, here, pltpu.roll(here, 1, 0))
            below = jnp.where(level_row == OLEV - 1, here, pltpu.roll(here, OROW - 1, 0))
            here = here + OCEAN_VERTICAL * (above + below - 2.0 * here)
            if force:
                here = here + ff[pl.ds(pl.multiple_of(u * OROW, OROW), OROW), :]
            st[rows, :] = jnp.where(level_row < OLEV, here, 0.0)
            return carry

        lax.fori_loop(1, NT - 1, tile, 0)

    spread(False)

    keep_up = jnp.where(a > 0, 1.0, 0.0).astype(F32)
    keep_down = jnp.where(a < n_atm - 1, 1.0, 0.0).astype(F32)
    sends = (sa0, sa1)
    takes = (ra0, ra1)
    packs = (pa0, pa1)
    backs = (ba0, ba1)

    def dynamics(g):
        f0, nf = GROUPS[g]
        n = nf * NLEV
        sub = lax.rem(iota((n, 128), 0), NLEV)
        diff = jnp.zeros((n, 128), F32)
        wind = jnp.zeros((n, 128), F32)
        for l in range(NLEV):
            diff = jnp.where(sub == l, ld_s[l], diff)
            wind = jnp.where(sub == l, lw_s[l], wind)
        coef[0, pl.ds(0, n), :] = 1.0 - 4.0 * diff
        coef[1, pl.ds(0, n), :] = diff
        coef[2, pl.ds(0, n), :] = diff - 0.5 * wind
        coef[3, pl.ds(0, n), :] = diff + 0.5 * wind
        for b in range(3):
            for r in range(ROWS):
                for q in range(QS):
                    piece = nb[b, pl.ds(f0 * NLEV * HSUB + 4 * q + r, n, stride=HSUB), :]
                    if b == 0:
                        piece = piece * keep_up
                    if b == 2:
                        piece = piece * keep_down
                    d0[b * ROWS + r, q, pl.ds(0, n), :] = piece
        lane = iota((n, 128), 1)
        bufs = (d0, d1)
        for step in range(1, DYN_STEPS + 1):
            src, dst = bufs[(step - 1) % 2], bufs[step % 2]

            def row(i, carry):
                here = [src[i, q, pl.ds(0, n), :] for q in range(QS)]
                to_east = [pltpu.roll(x, 1, 1) for x in here]
                to_west = [pltpu.roll(x, 127, 1) for x in here]
                for q in range(QS):
                    west = jnp.where(lane == 0, to_east[(q - 1) % QS], to_east[q])
                    east = jnp.where(lane == 127, to_west[(q + 1) % QS], to_west[q])
                    beside = src[i - 1, q, pl.ds(0, n), :] + src[i + 1, q, pl.ds(0, n), :]
                    new = (
                        coef[0, pl.ds(0, n), :] * here[q]
                        + coef[1, pl.ds(0, n), :] * beside
                        + coef[2, pl.ds(0, n), :] * east
                        + coef[3, pl.ds(0, n), :] * west
                    )
                    if step == DYN_STEPS:
                        sends[g][(i - ROWS) * 2 + q // 2, pl.ds((q % 2) * n, n), :] = new
                    else:
                        keep = jnp.where(i < ROWS, keep_up, jnp.where(i >= 2 * ROWS, keep_down, 1.0))
                        dst[i, q, pl.ds(0, n), :] = new * keep
                return carry

            lax.fori_loop(step, 3 * ROWS - step, row, 0)

    def exchange(src, dst, send, recv, g):
        copies = [
            remote(src.at[p], dst.at[o], send.at[g, p], recv.at[g, o], (a, p)) for p in peers
        ]
        own = pltpu.make_async_copy(src.at[o], dst.at[o], self_sem.at[g])
        for copy in copies:
            copy.start()
        own.start()
        arrivals = [
            remote(src.at[p], dst.at[p], send.at[g, p], recv.at[g, p], (a, p)) for p in peers
        ]
        return copies, own, arrivals

    def landed(handle):
        copies, own, arrivals = handle
        own.wait()
        for copy in arrivals:
            copy.wait_recv()

    out_there = []
    for g in range(2):
        for copy in halos[g]:
            copy.wait_recv()
        dynamics(g)
        out_there.append(exchange(sends[g], takes[g], a_send, a_recv, g))

    def physics(g):
        f0, nf = GROUPS[g]
        n = 2 * nf
        x = (xa, xb)[g]
        sub = iota((n, 128), 0)
        field = lax.rem(sub, nf)
        mix = jnp.zeros((n, 128), F32)
        rate = jnp.zeros((n, 128), F32)
        for f in range(nf):
            mix = jnp.where(field == f, vr_s[f0 + f], mix)
            rate = jnp.where(field == f, cr_s[f0 + f], rate)
        rate = rate * jnp.where(sub < nf, active[0], active[1])

        for lev in range(LEV):
            x[lev, pl.ds(0, n), :] = takes[g][lev // NLEV, pl.ds(lev % NLEV, n, stride=NLEV), :]

        def vertical(i, carry):
            here = x[0, pl.ds(0, n), :]
            above = here
            for lev in range(LEV):
                below = x[lev + 1, pl.ds(0, n), :] if lev < LEV - 1 else here
                x[lev, pl.ds(0, n), :] = here + mix * (above + below - 2.0 * here)
                above, here = here, below
            return carry

        lax.fori_loop(0, PHYS_ITERS, vertical, 0)

        def convect(i, carry):
            here = x[0, pl.ds(0, n), :]
            came = jnp.zeros((n, 128), F32)
            for lev in range(LEV - 1):
                below = x[lev + 1, pl.ds(0, n), :]
                transfer = rate * jnp.tanh(below - here)
                x[lev, pl.ds(0, n), :] = here + transfer - came
                came, here = transfer, below
            x[LEV - 1, pl.ds(0, n), :] = here - came
            return carry

        lax.fori_loop(0, CONV_ITERS, convect, 0)

    def pack(g):
        nf = GROUPS[g][1]
        n = 2 * nf
        x = (xa, xb)[g]
        for lev in range(LEV):
            packs[g][lev // NLEV, pl.ds(lev % NLEV, n, stride=NLEV), :] = x[lev, pl.ds(0, n), :]

    landed(out_there[0])
    physics(0)

    fl[...] = jnp.zeros((8, 128), F32)
    for half in range(2):
        low_row = [xa[LEV - 1, pl.ds(half * 4 + f, 1), :] for f in range(4)]
        speed = jnp.sqrt(1.0 + low_row[1] * low_row[1] + low_row[2] * low_row[2])
        heat = HEAT_COEF * speed * (low_row[0] - skin_v[pl.ds(half, 1), :])
        fresh = MOIST_COEF * speed * low_row[3]
        xa[LEV - 1, pl.ds(half * 4, 1), :] = low_row[0] - HEAT_BACK * heat
        xa[LEV - 1, pl.ds(half * 4 + 3, 1), :] = low_row[3] - MOIST_BACK * fresh
        fl[pl.ds(2 * half, 1), :] = heat
        fl[pl.ds(2 * half + 1, 1), :] = fresh
    fluxes = [
        remote(fl, fl_l, f_send.at[0], f_recv.at[0], right_id),
        remote(fl, fl_r, f_send.at[1], f_recv.at[1], left_id),
    ]
    for copy in fluxes:
        copy.start()
    pack(0)
    back_home = [exchange(packs[0], backs[0], b_send, b_recv, 0)]
    landed(out_there[1])
    physics(1)
    pack(1)
    back_home.append(exchange(packs[1], backs[1], b_send, b_recv, 1))

    for copy in fluxes:
        copy.wait_recv()
    near = jnp.concatenate(
        [
            fl_l[pl.ds(2, 1), :], fl[pl.ds(0, 1), :], fl[pl.ds(2, 1), :], fl_r[pl.ds(0, 1), :],
            fl_l[pl.ds(3, 1), :], fl[pl.ds(1, 1), :], fl[pl.ds(3, 1), :], fl_r[pl.ds(1, 1), :],
        ],
        axis=0,
    )
    sub8 = iota((8, 128), 0)
    chunk = lax.rem(sub8, 4)
    ff[...] = jnp.zeros(ff.shape, F32)
    for u in range(1, NT - 1):
        at = pl.ds(u * 128, 128)
        acc = jnp.zeros((8, 128), F32)
        for link in range(NW):
            source = fsrc_e[pl.ds(link, 1), at] - (dev * 256 - 128)
            source = jnp.broadcast_to(source, (8, 128))
            picked = jnp.take_along_axis(near, source & 127, axis=1, mode="promise_in_bounds")
            picked = jnp.where((source >> 7) == chunk, picked, 0.0)
            acc = acc + fw_e[pl.ds(link, 1), at] * picked
        ff[pl.ds(u * OROW, 1), :] = OCEAN_FORCE * jnp.sum(acc[0:4], axis=0, keepdims=True)
        ff[pl.ds(u * OROW + 24, 1), :] = OCEAN_FORCE * jnp.sum(acc[4:8], axis=0, keepdims=True)
    for u in range(1, NT - 1):
        for f in range(2):
            row = pl.ds(u * OROW + 24 * f, 1)
            st[row, :] = st[row, :] + ff[row, :]

    def ocean_step(i, carry):
        spread(True)
        return carry

    lax.fori_loop(1, OSTEPS, ocean_step, 0)

    for u in range(2, 10):
        for f in range(2):
            oout[pl.ds((u - 2) * 2 + f, OLEV, stride=16), :] = st[pl.ds(u * OROW + f * 24, OLEV), :]
    ocean_copy = pltpu.make_async_copy(oout, out_ocean, out_sem.at[0])
    ocean_copy.start()

    uu[...] = jnp.zeros(uu.shape, F32)
    for u in range(1, NT - 1):
        uu[pl.ds(u, 1), :] = st[pl.ds(u * OROW, 1), :]
    top = (uu[pl.ds(0, 8), :], uu[pl.ds(8, 8), :])
    for half in range(2):
        at = pl.ds(half * 128, 128)
        acc = jnp.zeros((8, 128), F32)
        for link in range(NW):
            source = ssrc_v[pl.ds(link, 1), at] - (dev * 1024 - 256)
            source = jnp.broadcast_to(source, (8, 128))
            weight = sw_v[pl.ds(link, 1), at]
            for part in range(2):
                picked = jnp.take_along_axis(top[part], source & 127, axis=1, mode="promise_in_bounds")
                picked = jnp.where((source >> 7) == sub8 + 8 * part, picked, 0.0)
                acc = acc + weight * picked
        sout[pl.ds(half, 1), :] = jnp.sum(acc, axis=0, keepdims=True)
    surf_copy = pltpu.make_async_copy(sout, out_surf, out_sem.at[1])
    surf_copy.start()

    out_copies = [ocean_copy, surf_copy]
    for g in range(2):
        f0, nf = GROUPS[g]
        n = nf * NLEV
        landed(back_home[g])
        for r in range(ROWS):
            for q in range(QS):
                piece = backs[g][2 * r + q // 2, pl.ds((q % 2) * n, n), :]
                out_v[pl.ds(f0 * NLEV * HSUB + 4 * q + r, n, stride=HSUB), :] = piece
        rows = pl.ds(f0 * NLEV * HSUB, n * HSUB)
        copy = pltpu.make_async_copy(out_v.at[rows], out_atm.at[rows], out_sem.at[2 + g])
        copy.start()
        out_copies.append(copy)

    for copy in halos[0] + halos[1] + edges + fluxes:
        copy.wait_send()
    for copies, own, arrivals in out_there + back_home:
        for copy in copies:
            copy.wait_send()
    for copy in out_copies:
        copy.wait()


def local(n_atm, n_ocn, atm_state, level_diffusion, level_wind, vertical_rate, convective_rate,
          ocean_skin, trigger, group_order, ocean_state, ocean_neighbors, flux_sources,
          flux_weights, surface_sources, surface_weights):
    atm = atm_state.reshape(FIELDS, NLEV, ROWS, QS, 128).transpose(0, 1, 3, 2, 4).reshape(1008, 128)
    ocean = ocean_state.transpose(1, 0, 2).reshape(OLEV, 2, 8, 128).transpose(0, 2, 1, 3).reshape(320, 128)
    hbm = pl.BlockSpec(memory_space=pltpu.HBM)
    dma = pltpu.SemaphoreType.DMA

    def vmem(*shape, dtype=F32):
        return pltpu.VMEM(shape, dtype)

    new_atm, new_ocean, surf = pl.pallas_call(
        functools.partial(kernel, n_atm, n_ocn),
        out_shape=(
            jax.ShapeDtypeStruct((1008, 128), F32),
            jax.ShapeDtypeStruct((320, 128), F32),
            jax.ShapeDtypeStruct((2, 128), F32),
        ),
        in_specs=[hbm] * 14,
        out_specs=(hbm,) * 3,
        scratch_shapes=[
            pltpu.SMEM((NLEV,), F32), pltpu.SMEM((NLEV,), F32),
            pltpu.SMEM((FIELDS,), F32), pltpu.SMEM((FIELDS,), F32),
            vmem(2, 128), vmem(2, 128, dtype=jnp.int32), vmem(2, 128, dtype=jnp.int32),
            vmem(4, 256, dtype=jnp.int32), vmem(4, 256),
            vmem(3, 1008, 128), vmem(12, QS, 40, 128), vmem(12, QS, 40, 128), vmem(4, 40, 128),
            vmem(8, 72, 128), vmem(8, 72, 128), vmem(8, 72, 128), vmem(8, 72, 128),
            vmem(8, 56, 128), vmem(8, 56, 128), vmem(8, 56, 128), vmem(8, 56, 128),
            vmem(LEV, 8, 128), vmem(LEV, 8, 128), vmem(1008, 128),
            vmem(160, 128), vmem(320, 128), vmem(160, 128),
            vmem(NBR, 1536, dtype=jnp.int32), vmem(NW, 1536, dtype=jnp.int32), vmem(NW, 1536),
            vmem(NT * OROW, 128), vmem(NT, PARTS * OROW, 128, dtype=BF16),
            vmem(NT - 2, 384, 128, dtype=BF16), vmem(NT * OROW, 128), vmem(16, 128),
            vmem(320, 128), vmem(2, 128),
            vmem(8, 128), vmem(8, 128), vmem(8, 128),
            dma((14,)), dma((2, 2)), dma((2, 2)), dma((8,)), dma((8,)),
            dma((2, 8)), dma((2, 8)), dma((2, 8)), dma((2, 8)), dma((2,)),
            dma((2,)), dma((2,)), dma((4,)),
        ],
        compiler_params=pltpu.CompilerParams(
            collective_id=0, has_side_effects=True, vmem_limit_bytes=40 * 1024 * 1024
        ),
    )(
        atm, level_diffusion, level_wind, vertical_rate, convective_rate,
        ocean_skin.reshape(2, 128), trigger.reshape(2, 128), group_order.reshape(2, 128),
        ocean, ocean_neighbors, flux_sources, flux_weights, surface_sources, surface_weights,
    )
    new_atm = new_atm.reshape(FIELDS, NLEV, QS, ROWS, 128).transpose(0, 1, 3, 2, 4)
    new_ocean = new_ocean.reshape(OLEV, 8, 2, 128).transpose(0, 2, 1, 3).reshape(OLEV, 2, 1024)
    return (
        new_atm.reshape(FIELDS, NLEV, ROWS, QS * 128),
        new_ocean.transpose(1, 0, 2),
        surf.reshape(256),
    )


def solution(mesh):
    both = ("atm", "ocn")
    return jax.shard_map(
        functools.partial(local, mesh.shape["atm"], mesh.shape["ocn"]),
        mesh=mesh,
        in_specs=(
            P(None, "ocn", "atm", None), P("ocn"), P("ocn"), P(), P(),
            P(both), P(both), P(both), P(None, None, both),
            P(None, both), P(None, both), P(None, both), P(None, both), P(None, both),
        ),
        out_specs=(P(None, "ocn", "atm", None), P(None, None, both), P(both)),
        check_vma=False,
    )
```

```python
import functools

import jax
import jax.numpy as jnp
from jax import lax
from jax.experimental import pallas as pl
from jax.experimental.pallas import tpu as pltpu
from jax.sharding import PartitionSpec as P

MESH = pl.DeviceIdType.MESH
F32 = jnp.float32
BF16 = jnp.bfloat16

FIELDS = 7
LEV = 72
NLEV = 9
ROWS = 4
QS = 4
DYN_STEPS = 4
PHYS_ITERS = 3
CONV_ITERS = 24
OLEV = 20
OSTEPS = 4
NBR = 6
NW = 4
PARTS = 3
OROW = 48
NT = 12
OCEAN_SPREAD = 0.6
OCEAN_VERTICAL = 0.2
HEAT_COEF = 0.5
MOIST_COEF = 0.5
HEAT_BACK = 0.3
MOIST_BACK = 0.3
OCEAN_FORCE = 0.3

GROUPS = ((0, 4), (4, 3))
HSUB = 16


def iota(shape, dim):
    return lax.broadcasted_iota(jnp.int32, shape, dim)


def kernel(
    n_atm,
    n_ocn,
    atm, ld, lw, vr, cr, skin, trig, order, ocean, nbr, fsrc, fw, ssrc, sw,
    ba0, ba1, out_ocean, out_surf,
    ld_s, lw_s, vr_s, cr_s, skin_v, trig_v, order_v, ssrc_v, sw_v,
    nb, d0, d1, coef,
    sa0, ra0, sc0, rc0, pa0, sa1, ra1, sc1, rc1, pa1,
    xa, xb,
    oc_o, nbr_e, fsrc_e, fw_e,
    st, hs, mm, ff, uu, oout, sout,
    fl, fl_l, fl_r,
    local_sem, halo_send, halo_recv, oh_send, oh_recv,
    a_send, a_recv, b_send, b_recv, c_send, c_recv, self_sem, f_send, f_recv, out_sem,
):
    a = lax.axis_index("atm")
    o = lax.axis_index("ocn")
    dev = a * n_ocn + o
    odd = lax.rem(a, 2)
    mate = a + 1 - 2 * odd
    cross = lax.rem(a + n_atm - 1 + 2 * odd, n_atm)
    total = n_atm * n_ocn
    left = lax.rem(dev + total - 1, total)
    right = lax.rem(dev + 1, total)
    left_id = (left // n_ocn, lax.rem(left, n_ocn))
    right_id = (right // n_ocn, lax.rem(right, n_ocn))
    peers = [lax.rem(o + d, n_ocn) for d in range(1, n_ocn)]

    fills = [
        (ld, ld_s), (lw, lw_s), (vr, vr_s), (cr, cr_s),
        (skin, skin_v), (trig, trig_v), (order, order_v), (ssrc, ssrc_v), (sw, sw_v),
        (atm, nb.at[0]), (ocean, oc_o),
        (nbr, nbr_e.at[:, pl.ds(256, 1024)]),
        (fsrc, fsrc_e.at[:, pl.ds(256, 1024)]),
        (fw, fw_e.at[:, pl.ds(256, 1024)]),
    ]
    fills = [
        pltpu.make_async_copy(src, dst, local_sem.at[i]) for i, (src, dst) in enumerate(fills)
    ]
    for copy in fills:
        copy.start()

    barrier = pltpu.get_barrier_semaphore()
    partners = [(mate, o), left_id, right_id, (cross, o)]
    partners += [(a, p) for p in peers] + [(cross, p) for p in peers]
    for partner in partners:
        pl.semaphore_signal(barrier, inc=1, device_id=partner, device_id_type=MESH)
    pl.semaphore_wait(barrier, len(partners))

    def remote(src, dst, send, recv, device):
        return pltpu.make_async_remote_copy(
            src_ref=src, dst_ref=dst, send_sem=send, recv_sem=recv,
            device_id=device, device_id_type=MESH,
        )

    halos = []
    for g, (f0, nf) in enumerate(GROUPS):
        rows = pl.ds(f0 * NLEV * HSUB, nf * NLEV * HSUB)
        copy = remote(atm.at[rows], nb.at[1, rows], halo_send.at[g], halo_recv.at[g], (mate, o))
        copy.start()
        halos.append(copy)
    for copy in fills:
        copy.wait()

    unused = jnp.zeros((4, 128), F32)
    for u in range(2, 10):
        for f in range(2):
            piece = oc_o[pl.ds((u - 2) * 2 + f, OLEV, stride=16), :]
            st[pl.ds(u * OROW + f * 24, OLEV), :] = piece
            st[pl.ds(u * OROW + f * 24 + OLEV, 4), :] = unused

    def tiles(u):
        return st.at[pl.ds(u * OROW, 2 * OROW)]

    last, first = pl.ds(896, 128), pl.ds(0, 128)
    low, high = pl.ds(128, 128), pl.ds(1280, 128)
    edge = [
        (tiles(8), tiles(0), right_id),
        (nbr.at[:, last], nbr_e.at[:, low], right_id),
        (fsrc.at[:, last], fsrc_e.at[:, low], right_id),
        (fw.at[:, last], fw_e.at[:, low], right_id),
        (tiles(2), tiles(10), left_id),
        (nbr.at[:, first], nbr_e.at[:, high], left_id),
        (fsrc.at[:, first], fsrc_e.at[:, high], left_id),
        (fw.at[:, first], fw_e.at[:, high], left_id),
    ]
    edges = [
        remote(src, dst, oh_send.at[i], oh_recv.at[i], device)
        for i, (src, dst, device) in enumerate(edge)
    ]
    for copy in edges:
        copy.start()

    edge_row = jnp.where(odd == 1, n_atm - 1, 0)
    keep = jnp.where(a == edge_row, 0.0, 1.0).astype(F32)
    sends = (sa0, sa1)
    takes = (ra0, ra1)
    gives = (sc0, sc1)
    adds = (rc0, rc1)
    packs = (pa0, pa1)
    backs = (ba0, ba1)

    def dynamics(g):
        f0, nf = GROUPS[g]
        n = nf * NLEV
        sub = lax.rem(iota((n, 128), 0), NLEV)
        diff = jnp.zeros((n, 128), F32)
        wind = jnp.zeros((n, 128), F32)
        for l in range(NLEV):
            diff = jnp.where(sub == l, ld_s[l], diff)
            wind = jnp.where(sub == l, lw_s[l], wind)
        coef[0, pl.ds(0, n), :] = 1.0 - 4.0 * diff
        coef[1, pl.ds(0, n), :] = diff
        coef[2, pl.ds(0, n), :] = diff - 0.5 * wind
        coef[3, pl.ds(0, n), :] = diff + 0.5 * wind
        none = jnp.zeros((n, 128), F32)
        for q in range(QS):
            for i in range(ROWS + 1):
                d0[i, q, pl.ds(0, n), :] = none
                d1[i, q, pl.ds(0, n), :] = none
            for b in range(2):
                block = [
                    nb[b, pl.ds(f0 * NLEV * HSUB + 4 * q + r, n, stride=HSUB), :] for r in range(ROWS)
                ]
                for r in range(ROWS):
                    piece = jnp.where(odd == 1, block[ROWS - 1 - r], block[r])
                    d0[1 + (b + 1) * ROWS + r, q, pl.ds(0, n), :] = piece
        lane = iota((n, 128), 1)
        bufs = (d0, d1)

        def update(src, i):
            here = [src[i, q, pl.ds(0, n), :] for q in range(QS)]
            to_east = [pltpu.roll(x, 1, 1) for x in here]
            to_west = [pltpu.roll(x, 127, 1) for x in here]
            new = []
            for q in range(QS):
                west = jnp.where(lane == 0, to_east[(q - 1) % QS], to_east[q])
                east = jnp.where(lane == 127, to_west[(q + 1) % QS], to_west[q])
                beside = src[i - 1, q, pl.ds(0, n), :] + src[i + 1, q, pl.ds(0, n), :]
                new.append(
                    coef[0, pl.ds(0, n), :] * here[q]
                    + coef[1, pl.ds(0, n), :] * beside
                    + coef[2, pl.ds(0, n), :] * east
                    + coef[3, pl.ds(0, n), :] * west
                )
            return new

        for step in range(1, DYN_STEPS):
            src, dst = bufs[(step - 1) % 2], bufs[step % 2]

            def row(i, carry):
                scale = jnp.where(i <= ROWS, keep, 1.0)
                for q, value in enumerate(update(src, i)):
                    dst[i, q, pl.ds(0, n), :] = value * scale
                return carry

            lax.fori_loop(1 + ROWS - step, 1 + 3 * ROWS - step, row, 0)

        src = bufs[(DYN_STEPS - 1) % 2]

        def last_row(dst, scale):
            def body(i, carry):
                r = jnp.where(odd == 1, ROWS - 1 - i, i)
                first = 1 if dst is gives[g] else 1 + ROWS
                for q, value in enumerate(update(src, i + first)):
                    if scale is not None:
                        value = value * scale
                    dst[r * 2 + q // 2, pl.ds((q % 2) * n, n), :] = value
                return carry

            return body

        lax.fori_loop(0, ROWS, last_row(gives[g], keep), 0)
        everyone = [o] + peers
        copies = [
            remote(gives[g].at[p], adds[g].at[o], c_send.at[g, p], c_recv.at[g, o], (cross, p))
            for p in everyone
        ]
        for copy in copies:
            copy.start()
        arrivals = [
            remote(gives[g].at[p], adds[g].at[p], c_send.at[g, p], c_recv.at[g, p], (cross, p))
            for p in everyone
        ]
        lax.fori_loop(0, ROWS, last_row(sends[g], None), 0)
        return copies, None, arrivals

    def exchange(src, dst, send, recv, own_sem, g):
        copies = [
            remote(src.at[p], dst.at[o], send.at[g, p], recv.at[g, o], (a, p)) for p in peers
        ]
        own = pltpu.make_async_copy(src.at[o], dst.at[o], own_sem)
        for copy in copies:
            copy.start()
        own.start()
        arrivals = [
            remote(src.at[p], dst.at[p], send.at[g, p], recv.at[g, p], (a, p)) for p in peers
        ]
        return copies, own, arrivals

    def landed(handle):
        copies, own, arrivals = handle
        if own is not None:
            own.wait()
        for copy in arrivals:
            copy.wait_recv()

    out_there = []
    out_cross = []
    for g in range(2):
        halos[g].wait_recv()
        out_cross.append(dynamics(g))
        out_there.append(exchange(sends[g], takes[g], a_send, a_recv, self_sem.at[g], g))

    hit = jnp.where(trig_v[...] > 0, order_v[...], -1).astype(F32)
    hit = jnp.concatenate([hit, jnp.full((6, 128), -1.0, F32)], axis=0)
    hit = jnp.transpose(hit, (1, 0))
    lane = iota((128, 128), 1)
    active = []
    for half in range(2):
        column = (lane + 128 * half).astype(F32)
        mark = jnp.where(hit[:, 0:1] == column, 1.0, 0.0) + jnp.where(hit[:, 1:2] == column, 1.0, 0.0)
        active.append(jnp.sum(mark, axis=0, keepdims=True))

    for copy in edges:
        copy.wait_recv()
    for copy in edges:
        copy.wait_send()

    def build(u, carry):
        at = pl.multiple_of(u * 128, 128)
        k = iota((192, 128), 0) + 96
        base = iota((1, 128), 1) + 128
        count = jnp.zeros((192, 128), F32)
        for j in range(NBR):
            target = nbr_e[pl.ds(j, 1), pl.ds(at, 128)] + base
            count = count + jnp.where(k == target, 1.0, 0.0)
        mm[u - 1, pl.ds(0, 96), :] = jnp.zeros((96, 128), BF16)
        mm[u - 1, pl.ds(96, 192), :] = count.astype(BF16)
        mm[u - 1, pl.ds(288, 96), :] = jnp.zeros((96, 128), BF16)
        return carry

    lax.fori_loop(1, NT - 1, build, 0)

    level_row = lax.rem(iota((OROW, 128), 0), 24)

    def spread(force):
        def split(u, carry):
            rest = st[pl.ds(pl.multiple_of(u * OROW, OROW), OROW), :]
            for part in range(PARTS):
                piece = rest.astype(BF16)
                hs[u, pl.ds(part * OROW, OROW), :] = piece
                rest = rest - piece.astype(F32)
            return carry

        lax.fori_loop(0, NT, split, 0)

        def tile(u, carry):
            source = jnp.concatenate([hs[u - 1], hs[u], hs[u + 1]], axis=1)
            sums = jnp.dot(source, mm[u - 1], preferred_element_type=F32)
            around = sums[0:OROW]
            for part in range(1, PARTS):
                around = around + sums[part * OROW : (part + 1) * OROW]
            rows = pl.ds(pl.multiple_of(u * OROW, OROW), OROW)
            here = st[rows, :]
            here = here + OCEAN_SPREAD * (around * (1.0 / 6.0) - here)
            above = jnp.where(level_row == 0, here, pltpu.roll(here, 1, 0))
            below = jnp.where(level_row == OLEV - 1, here, pltpu.roll(here, OROW - 1, 0))
            here = here + OCEAN_VERTICAL * (above + below - 2.0 * here)
            if force:
                here = here + ff[pl.ds(pl.multiple_of(u * OROW, OROW), OROW), :]
            st[rows, :] = jnp.where(level_row < OLEV, here, 0.0)
            return carry

        lax.fori_loop(1, NT - 1, tile, 0)

    spread(False)

    def physics(g):
        f0, nf = GROUPS[g]
        n = 2 * nf
        x = (xa, xb)[g]
        sub = iota((n, 128), 0)
        field = lax.rem(sub, nf)
        mix = jnp.zeros((n, 128), F32)
        rate = jnp.zeros((n, 128), F32)
        for f in range(nf):
            mix = jnp.where(field == f, vr_s[f0 + f], mix)
            rate = jnp.where(field == f, cr_s[f0 + f], rate)
        rate = rate * jnp.where(sub < nf, active[0], active[1])

        for lev in range(LEV):
            rows = pl.ds(lev % NLEV, n, stride=NLEV)
            x[lev, pl.ds(0, n), :] = takes[g][lev // NLEV, rows, :] + adds[g][lev // NLEV, rows, :]

        def vertical(i, carry):
            here = x[0, pl.ds(0, n), :]
            above = here
            for lev in range(LEV):
                below = x[lev + 1, pl.ds(0, n), :] if lev < LEV - 1 else here
                x[lev, pl.ds(0, n), :] = here + mix * (above + below - 2.0 * here)
                above, here = here, below
            return carry

        lax.fori_loop(0, PHYS_ITERS, vertical, 0)

        def convect(i, carry):
            here = x[0, pl.ds(0, n), :]
            came = jnp.zeros((n, 128), F32)
            for lev in range(LEV - 1):
                below = x[lev + 1, pl.ds(0, n), :]
                transfer = rate * jnp.tanh(below - here)
                x[lev, pl.ds(0, n), :] = here + transfer - came
                came, here = transfer, below
            x[LEV - 1, pl.ds(0, n), :] = here - came
            return carry

        lax.fori_loop(0, CONV_ITERS, convect, 0)

    def pack(g):
        nf = GROUPS[g][1]
        n = 2 * nf
        x = (xa, xb)[g]
        for lev in range(LEV):
            packs[g][lev // NLEV, pl.ds(lev % NLEV, n, stride=NLEV), :] = x[lev, pl.ds(0, n), :]

    landed(out_there[0])
    landed(out_cross[0])
    physics(0)

    fl[...] = jnp.zeros((8, 128), F32)
    for half in range(2):
        low_row = [xa[LEV - 1, pl.ds(half * 4 + f, 1), :] for f in range(4)]
        speed = jnp.sqrt(1.0 + low_row[1] * low_row[1] + low_row[2] * low_row[2])
        heat = HEAT_COEF * speed * (low_row[0] - skin_v[pl.ds(half, 1), :])
        fresh = MOIST_COEF * speed * low_row[3]
        xa[LEV - 1, pl.ds(half * 4, 1), :] = low_row[0] - HEAT_BACK * heat
        xa[LEV - 1, pl.ds(half * 4 + 3, 1), :] = low_row[3] - MOIST_BACK * fresh
        fl[pl.ds(2 * half, 1), :] = heat
        fl[pl.ds(2 * half + 1, 1), :] = fresh
    fluxes = [
        remote(fl, fl_l, f_send.at[0], f_recv.at[0], right_id),
        remote(fl, fl_r, f_send.at[1], f_recv.at[1], left_id),
    ]
    for copy in fluxes:
        copy.start()
    pack(0)
    back_home = [exchange(packs[0], backs[0], b_send, b_recv, self_sem.at[2], 0)]
    landed(out_there[1])
    landed(out_cross[1])
    physics(1)
    pack(1)
    back_home.append(exchange(packs[1], backs[1], b_send, b_recv, self_sem.at[3], 1))

    for copy in fluxes:
        copy.wait_recv()
    near = jnp.concatenate(
        [
            fl_l[pl.ds(2, 1), :], fl[pl.ds(0, 1), :], fl[pl.ds(2, 1), :], fl_r[pl.ds(0, 1), :],
            fl_l[pl.ds(3, 1), :], fl[pl.ds(1, 1), :], fl[pl.ds(3, 1), :], fl_r[pl.ds(1, 1), :],
        ],
        axis=0,
    )
    sub8 = iota((8, 128), 0)
    chunk = lax.rem(sub8, 4)
    ff[...] = jnp.zeros(ff.shape, F32)
    for u in range(1, NT - 1):
        at = pl.ds(u * 128, 128)
        acc = jnp.zeros((8, 128), F32)
        for link in range(NW):
            source = fsrc_e[pl.ds(link, 1), at] - (dev * 256 - 128)
            source = jnp.broadcast_to(source, (8, 128))
            picked = jnp.take_along_axis(near, source & 127, axis=1, mode="promise_in_bounds")
            picked = jnp.where((source >> 7) == chunk, picked, 0.0)
            acc = acc + fw_e[pl.ds(link, 1), at] * picked
        ff[pl.ds(u * OROW, 1), :] = OCEAN_FORCE * jnp.sum(acc[0:4], axis=0, keepdims=True)
        ff[pl.ds(u * OROW + 24, 1), :] = OCEAN_FORCE * jnp.sum(acc[4:8], axis=0, keepdims=True)
    for u in range(1, NT - 1):
        for f in range(2):
            row = pl.ds(u * OROW + 24 * f, 1)
            st[row, :] = st[row, :] + ff[row, :]

    def ocean_step(i, carry):
        spread(True)
        return carry

    lax.fori_loop(1, OSTEPS, ocean_step, 0)

    for u in range(2, 10):
        for f in range(2):
            oout[pl.ds((u - 2) * 2 + f, OLEV, stride=16), :] = st[pl.ds(u * OROW + f * 24, OLEV), :]
    ocean_copy = pltpu.make_async_copy(oout, out_ocean, out_sem.at[0])
    ocean_copy.start()

    uu[...] = jnp.zeros(uu.shape, F32)
    for u in range(1, NT - 1):
        uu[pl.ds(u, 1), :] = st[pl.ds(u * OROW, 1), :]
    top = (uu[pl.ds(0, 8), :], uu[pl.ds(8, 8), :])
    for half in range(2):
        at = pl.ds(half * 128, 128)
        acc = jnp.zeros((8, 128), F32)
        for link in range(NW):
            source = ssrc_v[pl.ds(link, 1), at] - (dev * 1024 - 256)
            source = jnp.broadcast_to(source, (8, 128))
            weight = sw_v[pl.ds(link, 1), at]
            for part in range(2):
                picked = jnp.take_along_axis(top[part], source & 127, axis=1, mode="promise_in_bounds")
                picked = jnp.where((source >> 7) == sub8 + 8 * part, picked, 0.0)
                acc = acc + weight * picked
        sout[pl.ds(half, 1), :] = jnp.sum(acc, axis=0, keepdims=True)
    surf_copy = pltpu.make_async_copy(sout, out_surf, out_sem.at[1])
    surf_copy.start()

    for handle in back_home:
        landed(handle)
    for copy in halos + fluxes:
        copy.wait_send()
    for copies, own, arrivals in out_there + out_cross + back_home:
        for copy in copies:
            copy.wait_send()
    ocean_copy.wait()
    surf_copy.wait()


def finish(ba0, ba1, ocean, surf, out_atm, out_ocean, out_surf, b0, b1, ocean_v, surf_v, out_v, sem):
    ins = ((ba0, b0), (ba1, b1), (ocean, ocean_v), (surf, surf_v))
    copies = [pltpu.make_async_copy(src, dst, sem.at[i]) for i, (src, dst) in enumerate(ins)]
    for copy in copies:
        copy.start()
    outs = []
    for g, (f0, nf) in enumerate(GROUPS):
        n = nf * NLEV
        copies[g].wait()
        for r in range(ROWS):
            for q in range(QS):
                piece = (b0, b1)[g][2 * r + q // 2, pl.ds((q % 2) * n, n), :]
                out_v[pl.ds(f0 * NLEV * HSUB + 4 * q + r, n, stride=HSUB), :] = piece
        rows = pl.ds(f0 * NLEV * HSUB, n * HSUB)
        outs.append(pltpu.make_async_copy(out_v.at[rows], out_atm.at[rows], sem.at[4 + g]))
        outs[-1].start()
    for i, (src, dst) in enumerate(((ocean_v, out_ocean), (surf_v, out_surf))):
        copies[2 + i].wait()
        outs.append(pltpu.make_async_copy(src, dst, sem.at[6 + i]))
        outs[-1].start()
    for copy in outs:
        copy.wait()


def local(n_atm, n_ocn, atm_state, level_diffusion, level_wind, vertical_rate, convective_rate,
          ocean_skin, trigger, group_order, ocean_state, ocean_neighbors, flux_sources,
          flux_weights, surface_sources, surface_weights):
    atm = atm_state.reshape(FIELDS, NLEV, ROWS, QS, 128).transpose(0, 1, 3, 2, 4).reshape(1008, 128)
    ocean = ocean_state.transpose(1, 0, 2).reshape(OLEV, 2, 8, 128).transpose(0, 2, 1, 3).reshape(320, 128)
    hbm = pl.BlockSpec(memory_space=pltpu.HBM)
    dma = pltpu.SemaphoreType.DMA

    def vmem(*shape, dtype=F32):
        return pltpu.VMEM(shape, dtype)

    parts = pl.pallas_call(
        functools.partial(kernel, n_atm, n_ocn),
        out_shape=(
            jax.ShapeDtypeStruct((8, 72, 128), F32),
            jax.ShapeDtypeStruct((8, 56, 128), F32),
            jax.ShapeDtypeStruct((320, 128), F32),
            jax.ShapeDtypeStruct((2, 128), F32),
        ),
        in_specs=[hbm] * 14,
        out_specs=(hbm,) * 4,
        scratch_shapes=[
            pltpu.SMEM((NLEV,), F32), pltpu.SMEM((NLEV,), F32),
            pltpu.SMEM((FIELDS,), F32), pltpu.SMEM((FIELDS,), F32),
            vmem(2, 128), vmem(2, 128, dtype=jnp.int32), vmem(2, 128, dtype=jnp.int32),
            vmem(4, 256, dtype=jnp.int32), vmem(4, 256),
            vmem(2, 1008, 128), vmem(13, QS, 40, 128), vmem(13, QS, 40, 128), vmem(4, 40, 128),
            *[vmem(8, 72, 128)] * 5, *[vmem(8, 56, 128)] * 5,
            vmem(LEV, 8, 128), vmem(LEV, 8, 128),
            vmem(320, 128),
            vmem(NBR, 1536, dtype=jnp.int32), vmem(NW, 1536, dtype=jnp.int32), vmem(NW, 1536),
            vmem(NT * OROW, 128), vmem(NT, PARTS * OROW, 128, dtype=BF16),
            vmem(NT - 2, 384, 128, dtype=BF16), vmem(NT * OROW, 128), vmem(16, 128),
            vmem(320, 128), vmem(2, 128),
            vmem(8, 128), vmem(8, 128), vmem(8, 128),
            dma((14,)), dma((2,)), dma((2,)), dma((8,)), dma((8,)),
            dma((2, 8)), dma((2, 8)), dma((2, 8)), dma((2, 8)), dma((2, 8)), dma((2, 8)), dma((4,)),
            dma((2,)), dma((2,)), dma((2,)),
        ],
        compiler_params=pltpu.CompilerParams(
            collective_id=0, has_side_effects=True, vmem_limit_bytes=60 * 1024 * 1024
        ),
    )(
        atm, level_diffusion, level_wind, vertical_rate, convective_rate,
        ocean_skin.reshape(2, 128), trigger.reshape(2, 128), group_order.reshape(2, 128),
        ocean, ocean_neighbors, flux_sources, flux_weights, surface_sources, surface_weights,
    )
    new_atm, new_ocean, surf = pl.pallas_call(
        finish,
        out_shape=(
            jax.ShapeDtypeStruct((1008, 128), F32),
            jax.ShapeDtypeStruct((320, 128), F32),
            jax.ShapeDtypeStruct((2, 128), F32),
        ),
        in_specs=[hbm] * 4,
        out_specs=(hbm,) * 3,
        scratch_shapes=[
            vmem(8, 72, 128), vmem(8, 56, 128), vmem(320, 128), vmem(2, 128), vmem(1008, 128), dma((8,)),
        ],
        compiler_params=pltpu.CompilerParams(vmem_limit_bytes=60 * 1024 * 1024),
    )(*parts)
    new_atm = new_atm.reshape(FIELDS, NLEV, QS, ROWS, 128).transpose(0, 1, 3, 2, 4)
    new_ocean = new_ocean.reshape(OLEV, 8, 2, 128).transpose(0, 2, 1, 3).reshape(OLEV, 2, 1024)
    return (
        new_atm.reshape(FIELDS, NLEV, ROWS, QS * 128),
        new_ocean.transpose(1, 0, 2),
        surf.reshape(256),
    )


def solution(mesh):
    both = ("atm", "ocn")
    return jax.shard_map(
        functools.partial(local, mesh.shape["atm"], mesh.shape["ocn"]),
        mesh=mesh,
        in_specs=(
            P(None, "ocn", "atm", None), P("ocn"), P("ocn"), P(), P(),
            P(both), P(both), P(both), P(None, None, both),
            P(None, both), P(None, both), P(None, both), P(None, both), P(None, both),
        ),
        out_specs=(P(None, "ocn", "atm", None), P(None, None, both), P(both)),
        check_vma=False,
    )
```

```python
import functools

import jax
import jax.numpy as jnp
from jax import lax
from jax.experimental import pallas as pl
from jax.experimental.pallas import tpu as pltpu
from jax.sharding import PartitionSpec as P

MESH = pl.DeviceIdType.MESH
F32 = jnp.float32
BF16 = jnp.bfloat16

FIELDS = 7
LEV = 72
NLEV = 9
ROWS = 4
QS = 4
DYN_STEPS = 4
PHYS_ITERS = 3
CONV_ITERS = 24
OLEV = 20
OSTEPS = 4
NBR = 6
NW = 4
PARTS = 3
OROW = 48
NT = 12
OCEAN_SPREAD = 0.6
OCEAN_VERTICAL = 0.2
HEAT_COEF = 0.5
MOIST_COEF = 0.5
HEAT_BACK = 0.3
MOIST_BACK = 0.3
OCEAN_FORCE = 0.3

GROUPS = ((0, 4), (4, 3))
HSUB = 16


def iota(shape, dim):
    return lax.broadcasted_iota(jnp.int32, shape, dim)


def kernel(
    n_atm,
    n_ocn,
    atm, ld, lw, vr, cr, skin, trig, order, ocean, nbr, fsrc, fw, ssrc, sw,
    ba0, ba1, out_ocean, out_surf,
    ld_s, lw_s, vr_s, cr_s, skin_v, trig_v, order_v, ssrc_v, sw_v,
    nb, d0, d1, coef,
    sa0, ra0, sc0, rc0, pa0, sa1, ra1, sc1, rc1, pa1,
    xa, xb,
    oc_o, nbr_e, fsrc_e, fw_e,
    st, hs, mm, ff, uu, oout, sout,
    fl, fl_l, fl_r,
    local_sem, halo_send, halo_recv, oh_send, oh_recv,
    a_send, a_recv, b_send, b_recv, c_send, c_recv, self_sem, f_send, f_recv, out_sem,
):
    a = lax.axis_index("atm")
    o = lax.axis_index("ocn")
    dev = a * n_ocn + o
    odd = lax.rem(a, 2)
    mate = a + 1 - 2 * odd
    cross = lax.rem(a + n_atm - 1 + 2 * odd, n_atm)
    total = n_atm * n_ocn
    left = lax.rem(dev + total - 1, total)
    right = lax.rem(dev + 1, total)
    left_id = (left // n_ocn, lax.rem(left, n_ocn))
    right_id = (right // n_ocn, lax.rem(right, n_ocn))
    peers = [lax.rem(o + d, n_ocn) for d in range(1, n_ocn)]

    fills = [
        (ld, ld_s), (lw, lw_s), (vr, vr_s), (cr, cr_s),
        (skin, skin_v), (trig, trig_v), (order, order_v), (ssrc, ssrc_v), (sw, sw_v),
        (atm, nb.at[0]), (ocean, oc_o),
        (nbr, nbr_e.at[:, pl.ds(256, 1024)]),
        (fsrc, fsrc_e.at[:, pl.ds(256, 1024)]),
        (fw, fw_e.at[:, pl.ds(256, 1024)]),
    ]
    fills = [
        pltpu.make_async_copy(src, dst, local_sem.at[i]) for i, (src, dst) in enumerate(fills)
    ]
    for copy in fills:
        copy.start()

    barrier = pltpu.get_barrier_semaphore()
    partners = [(mate, o), left_id, right_id, (cross, o)]
    partners += [(a, p) for p in peers] + [(cross, p) for p in peers]
    for partner in partners:
        pl.semaphore_signal(barrier, inc=1, device_id=partner, device_id_type=MESH)
    pl.semaphore_wait(barrier, len(partners))

    def remote(src, dst, send, recv, device):
        return pltpu.make_async_remote_copy(
            src_ref=src, dst_ref=dst, send_sem=send, recv_sem=recv,
            device_id=device, device_id_type=MESH,
        )

    halos = []
    for g, (f0, nf) in enumerate(GROUPS):
        rows = pl.ds(f0 * NLEV * HSUB, nf * NLEV * HSUB)
        copy = remote(atm.at[rows], nb.at[1, rows], halo_send.at[g], halo_recv.at[g], (mate, o))
        copy.start()
        halos.append(copy)
    for copy in fills:
        copy.wait()

    unused = jnp.zeros((4, 128), F32)
    for u in range(2, 10):
        for f in range(2):
            piece = oc_o[pl.ds((u - 2) * 2 + f, OLEV, stride=16), :]
            st[pl.ds(u * OROW + f * 24, OLEV), :] = piece
            st[pl.ds(u * OROW + f * 24 + OLEV, 4), :] = unused

    def tiles(u):
        return st.at[pl.ds(u * OROW, 2 * OROW)]

    last, first = pl.ds(896, 128), pl.ds(0, 128)
    low, high = pl.ds(128, 128), pl.ds(1280, 128)
    edge = [
        (tiles(8), tiles(0), right_id),
        (nbr.at[:, last], nbr_e.at[:, low], right_id),
        (fsrc.at[:, last], fsrc_e.at[:, low], right_id),
        (fw.at[:, last], fw_e.at[:, low], right_id),
        (tiles(2), tiles(10), left_id),
        (nbr.at[:, first], nbr_e.at[:, high], left_id),
        (fsrc.at[:, first], fsrc_e.at[:, high], left_id),
        (fw.at[:, first], fw_e.at[:, high], left_id),
    ]
    edges = [
        remote(src, dst, oh_send.at[i], oh_recv.at[i], device)
        for i, (src, dst, device) in enumerate(edge)
    ]
    for copy in edges:
        copy.start()

    edge_row = jnp.where(odd == 1, n_atm - 1, 0)
    keep = jnp.where(a == edge_row, 0.0, 1.0).astype(F32)
    sends = (sa0, sa1)
    takes = (ra0, ra1)
    gives = (sc0, sc1)
    adds = (rc0, rc1)
    packs = (pa0, pa1)
    backs = (ba0, ba1)

    def dynamics(g):
        f0, nf = GROUPS[g]
        n = nf * NLEV
        sub = lax.rem(iota((n, 128), 0), NLEV)
        diff = jnp.zeros((n, 128), F32)
        wind = jnp.zeros((n, 128), F32)
        for l in range(NLEV):
            diff = jnp.where(sub == l, ld_s[l], diff)
            wind = jnp.where(sub == l, lw_s[l], wind)
        coef[0, pl.ds(0, n), :] = 1.0 - 4.0 * diff
        coef[1, pl.ds(0, n), :] = diff
        coef[2, pl.ds(0, n), :] = diff - 0.5 * wind
        coef[3, pl.ds(0, n), :] = diff + 0.5 * wind
        none = jnp.zeros((n, 128), F32)
        for q in range(QS):
            for i in range(ROWS + 1):
                d0[i, q, pl.ds(0, n), :] = none
                d1[i, q, pl.ds(0, n), :] = none
            for b in range(2):
                block = [
                    nb[b, pl.ds(f0 * NLEV * HSUB + 4 * q + r, n, stride=HSUB), :] for r in range(ROWS)
                ]
                for r in range(ROWS):
                    piece = jnp.where(odd == 1, block[ROWS - 1 - r], block[r])
                    d0[1 + (b + 1) * ROWS + r, q, pl.ds(0, n), :] = piece
        lane = iota((n, 128), 1)
        bufs = (d0, d1)

        def update(src, i):
            here = [src[i, q, pl.ds(0, n), :] for q in range(QS)]
            to_east = [pltpu.roll(x, 1, 1) for x in here]
            to_west = [pltpu.roll(x, 127, 1) for x in here]
            new = []
            for q in range(QS):
                west = jnp.where(lane == 0, to_east[(q - 1) % QS], to_east[q])
                east = jnp.where(lane == 127, to_west[(q + 1) % QS], to_west[q])
                beside = src[i - 1, q, pl.ds(0, n), :] + src[i + 1, q, pl.ds(0, n), :]
                new.append(
                    coef[0, pl.ds(0, n), :] * here[q]
                    + coef[1, pl.ds(0, n), :] * beside
                    + coef[2, pl.ds(0, n), :] * east
                    + coef[3, pl.ds(0, n), :] * west
                )
            return new

        for step in range(1, DYN_STEPS):
            src, dst = bufs[(step - 1) % 2], bufs[step % 2]

            def row(i, carry):
                scale = jnp.where(i <= ROWS, keep, 1.0)
                for q, value in enumerate(update(src, i)):
                    dst[i, q, pl.ds(0, n), :] = value * scale
                return carry

            lax.fori_loop(1 + ROWS - step, 1 + 3 * ROWS - step, row, 0, unroll=True)

        src = bufs[(DYN_STEPS - 1) % 2]

        def last_row(dst, scale):
            def body(i, carry):
                r = jnp.where(odd == 1, ROWS - 1 - i, i)
                first = 1 if dst is gives[g] else 1 + ROWS
                for q, value in enumerate(update(src, i + first)):
                    if scale is not None:
                        value = value * scale
                    dst[r * 2 + q // 2, pl.ds((q % 2) * n, n), :] = value
                return carry

            return body

        lax.fori_loop(0, ROWS, last_row(gives[g], keep), 0, unroll=True)
        everyone = [o] + peers
        copies = [
            remote(gives[g].at[p], adds[g].at[o], c_send.at[g, p], c_recv.at[g, o], (cross, p))
            for p in everyone
        ]
        for copy in copies:
            copy.start()
        arrivals = [
            remote(gives[g].at[p], adds[g].at[p], c_send.at[g, p], c_recv.at[g, p], (cross, p))
            for p in everyone
        ]
        lax.fori_loop(0, ROWS, last_row(sends[g], None), 0, unroll=True)
        return copies, None, arrivals

    def exchange(src, dst, send, recv, own_sem, g):
        copies = [
            remote(src.at[p], dst.at[o], send.at[g, p], recv.at[g, o], (a, p)) for p in peers
        ]
        own = pltpu.make_async_copy(src.at[o], dst.at[o], own_sem)
        for copy in copies:
            copy.start()
        own.start()
        arrivals = [
            remote(src.at[p], dst.at[p], send.at[g, p], recv.at[g, p], (a, p)) for p in peers
        ]
        return copies, own, arrivals

    def landed(handle):
        copies, own, arrivals = handle
        if own is not None:
            own.wait()
        for copy in arrivals:
            copy.wait_recv()

    out_there = []
    out_cross = []
    for g in range(2):
        halos[g].wait_recv()
        out_cross.append(dynamics(g))
        out_there.append(exchange(sends[g], takes[g], a_send, a_recv, self_sem.at[g], g))

    hit = jnp.where(trig_v[...] > 0, order_v[...], -1).astype(F32)
    hit = jnp.concatenate([hit, jnp.full((6, 128), -1.0, F32)], axis=0)
    hit = jnp.transpose(hit, (1, 0))
    lane = iota((128, 128), 1)
    active = []
    for half in range(2):
        column = (lane + 128 * half).astype(F32)
        mark = jnp.where(hit[:, 0:1] == column, 1.0, 0.0) + jnp.where(hit[:, 1:2] == column, 1.0, 0.0)
        active.append(jnp.sum(mark, axis=0, keepdims=True))

    for copy in edges:
        copy.wait_recv()
    for copy in edges:
        copy.wait_send()

    def build(u, carry):
        at = pl.multiple_of(u * 128, 128)
        k = iota((192, 128), 0) + 96
        base = iota((1, 128), 1) + 128
        count = jnp.zeros((192, 128), F32)
        for j in range(NBR):
            target = nbr_e[pl.ds(j, 1), pl.ds(at, 128)] + base
            count = count + jnp.where(k == target, 1.0, 0.0)
        mm[u - 1, pl.ds(0, 96), :] = jnp.zeros((96, 128), BF16)
        mm[u - 1, pl.ds(96, 192), :] = count.astype(BF16)
        mm[u - 1, pl.ds(288, 96), :] = jnp.zeros((96, 128), BF16)
        return carry

    lax.fori_loop(1, NT - 1, build, 0, unroll=True)

    level_row = lax.rem(iota((OROW, 128), 0), 24)

    def spread(force):
        def split(u, carry):
            rest = st[pl.ds(pl.multiple_of(u * OROW, OROW), OROW), :]
            for part in range(PARTS):
                piece = rest.astype(BF16)
                hs[u, pl.ds(part * OROW, OROW), :] = piece
                rest = rest - piece.astype(F32)
            return carry

        lax.fori_loop(0, NT, split, 0, unroll=True)

        def tile(u, carry):
            source = jnp.concatenate([hs[u - 1], hs[u], hs[u + 1]], axis=1)
            sums = jnp.dot(source, mm[u - 1], preferred_element_type=F32)
            around = sums[0:OROW]
            for part in range(1, PARTS):
                around = around + sums[part * OROW : (part + 1) * OROW]
            rows = pl.ds(pl.multiple_of(u * OROW, OROW), OROW)
            here = st[rows, :]
            here = here + OCEAN_SPREAD * (around * (1.0 / 6.0) - here)
            above = jnp.where(level_row == 0, here, pltpu.roll(here, 1, 0))
            below = jnp.where(level_row == OLEV - 1, here, pltpu.roll(here, OROW - 1, 0))
            here = here + OCEAN_VERTICAL * (above + below - 2.0 * here)
            if force:
                here = here + ff[pl.ds(pl.multiple_of(u * OROW, OROW), OROW), :]
            st[rows, :] = jnp.where(level_row < OLEV, here, 0.0)
            return carry

        lax.fori_loop(1, NT - 1, tile, 0, unroll=True)

    spread(False)

    def physics(g):
        f0, nf = GROUPS[g]
        n = 2 * nf
        x = (xa, xb)[g]
        sub = iota((n, 128), 0)
        field = lax.rem(sub, nf)
        mix = jnp.zeros((n, 128), F32)
        rate = jnp.zeros((n, 128), F32)
        for f in range(nf):
            mix = jnp.where(field == f, vr_s[f0 + f], mix)
            rate = jnp.where(field == f, cr_s[f0 + f], rate)
        rate = rate * jnp.where(sub < nf, active[0], active[1])

        for lev in range(LEV):
            rows = pl.ds(lev % NLEV, n, stride=NLEV)
            x[lev, pl.ds(0, n), :] = takes[g][lev // NLEV, rows, :] + adds[g][lev // NLEV, rows, :]

        def vertical(i, carry):
            here = x[0, pl.ds(0, n), :]
            above = here
            for lev in range(LEV):
                below = x[lev + 1, pl.ds(0, n), :] if lev < LEV - 1 else here
                x[lev, pl.ds(0, n), :] = here + mix * (above + below - 2.0 * here)
                above, here = here, below
            return carry

        lax.fori_loop(0, PHYS_ITERS, vertical, 0)

        def convect(i, carry):
            here = x[0, pl.ds(0, n), :]
            came = jnp.zeros((n, 128), F32)
            for lev in range(LEV - 1):
                below = x[lev + 1, pl.ds(0, n), :]
                transfer = rate * jnp.tanh(below - here)
                x[lev, pl.ds(0, n), :] = here + transfer - came
                came, here = transfer, below
            x[LEV - 1, pl.ds(0, n), :] = here - came
            return carry

        lax.fori_loop(0, CONV_ITERS, convect, 0)

    def pack(g):
        nf = GROUPS[g][1]
        n = 2 * nf
        x = (xa, xb)[g]
        for lev in range(LEV):
            packs[g][lev // NLEV, pl.ds(lev % NLEV, n, stride=NLEV), :] = x[lev, pl.ds(0, n), :]

    landed(out_there[0])
    landed(out_cross[0])
    physics(0)

    fl[...] = jnp.zeros((8, 128), F32)
    for half in range(2):
        low_row = [xa[LEV - 1, pl.ds(half * 4 + f, 1), :] for f in range(4)]
        speed = jnp.sqrt(1.0 + low_row[1] * low_row[1] + low_row[2] * low_row[2])
        heat = HEAT_COEF * speed * (low_row[0] - skin_v[pl.ds(half, 1), :])
        fresh = MOIST_COEF * speed * low_row[3]
        xa[LEV - 1, pl.ds(half * 4, 1), :] = low_row[0] - HEAT_BACK * heat
        xa[LEV - 1, pl.ds(half * 4 + 3, 1), :] = low_row[3] - MOIST_BACK * fresh
        fl[pl.ds(2 * half, 1), :] = heat
        fl[pl.ds(2 * half + 1, 1), :] = fresh
    fluxes = [
        remote(fl, fl_l, f_send.at[0], f_recv.at[0], right_id),
        remote(fl, fl_r, f_send.at[1], f_recv.at[1], left_id),
    ]
    for copy in fluxes:
        copy.start()
    pack(0)
    back_home = [exchange(packs[0], backs[0], b_send, b_recv, self_sem.at[2], 0)]
    landed(out_there[1])
    landed(out_cross[1])
    physics(1)
    pack(1)
    back_home.append(exchange(packs[1], backs[1], b_send, b_recv, self_sem.at[3], 1))

    for copy in fluxes:
        copy.wait_recv()
    near = jnp.concatenate(
        [
            fl_l[pl.ds(2, 1), :], fl[pl.ds(0, 1), :], fl[pl.ds(2, 1), :], fl_r[pl.ds(0, 1), :],
            fl_l[pl.ds(3, 1), :], fl[pl.ds(1, 1), :], fl[pl.ds(3, 1), :], fl_r[pl.ds(1, 1), :],
        ],
        axis=0,
    )
    sub8 = iota((8, 128), 0)
    chunk = lax.rem(sub8, 4)
    ff[...] = jnp.zeros(ff.shape, F32)
    for u in range(1, NT - 1):
        at = pl.ds(u * 128, 128)
        acc = jnp.zeros((8, 128), F32)
        for link in range(NW):
            source = fsrc_e[pl.ds(link, 1), at] - (dev * 256 - 128)
            source = jnp.broadcast_to(source, (8, 128))
            picked = jnp.take_along_axis(near, source & 127, axis=1, mode="promise_in_bounds")
            picked = jnp.where((source >> 7) == chunk, picked, 0.0)
            acc = acc + fw_e[pl.ds(link, 1), at] * picked
        ff[pl.ds(u * OROW, 1), :] = OCEAN_FORCE * jnp.sum(acc[0:4], axis=0, keepdims=True)
        ff[pl.ds(u * OROW + 24, 1), :] = OCEAN_FORCE * jnp.sum(acc[4:8], axis=0, keepdims=True)
    for u in range(1, NT - 1):
        for f in range(2):
            row = pl.ds(u * OROW + 24 * f, 1)
            st[row, :] = st[row, :] + ff[row, :]

    def ocean_step(i, carry):
        spread(True)
        return carry

    lax.fori_loop(1, OSTEPS, ocean_step, 0)

    for u in range(2, 10):
        for f in range(2):
            oout[pl.ds((u - 2) * 2 + f, OLEV, stride=16), :] = st[pl.ds(u * OROW + f * 24, OLEV), :]
    ocean_copy = pltpu.make_async_copy(oout, out_ocean, out_sem.at[0])
    ocean_copy.start()

    uu[...] = jnp.zeros(uu.shape, F32)
    for u in range(1, NT - 1):
        uu[pl.ds(u, 1), :] = st[pl.ds(u * OROW, 1), :]
    top = (uu[pl.ds(0, 8), :], uu[pl.ds(8, 8), :])
    for half in range(2):
        at = pl.ds(half * 128, 128)
        acc = jnp.zeros((8, 128), F32)
        for link in range(NW):
            source = ssrc_v[pl.ds(link, 1), at] - (dev * 1024 - 256)
            source = jnp.broadcast_to(source, (8, 128))
            weight = sw_v[pl.ds(link, 1), at]
            for part in range(2):
                picked = jnp.take_along_axis(top[part], source & 127, axis=1, mode="promise_in_bounds")
                picked = jnp.where((source >> 7) == sub8 + 8 * part, picked, 0.0)
                acc = acc + weight * picked
        sout[pl.ds(half, 1), :] = jnp.sum(acc, axis=0, keepdims=True)
    surf_copy = pltpu.make_async_copy(sout, out_surf, out_sem.at[1])
    surf_copy.start()

    for handle in back_home:
        landed(handle)
    for copy in halos + fluxes:
        copy.wait_send()
    for copies, own, arrivals in out_there + out_cross + back_home:
        for copy in copies:
            copy.wait_send()
    ocean_copy.wait()
    surf_copy.wait()


def finish(ba0, ba1, ocean, surf, out_atm, out_ocean, out_surf, b0, b1, ocean_v, surf_v, out_v, sem):
    ins = ((ba0, b0), (ba1, b1), (ocean, ocean_v), (surf, surf_v))
    copies = [pltpu.make_async_copy(src, dst, sem.at[i]) for i, (src, dst) in enumerate(ins)]
    for copy in copies:
        copy.start()
    outs = []
    for g, (f0, nf) in enumerate(GROUPS):
        n = nf * NLEV
        copies[g].wait()
        for r in range(ROWS):
            for q in range(QS):
                piece = (b0, b1)[g][2 * r + q // 2, pl.ds((q % 2) * n, n), :]
                out_v[pl.ds(f0 * NLEV * HSUB + 4 * q + r, n, stride=HSUB), :] = piece
        rows = pl.ds(f0 * NLEV * HSUB, n * HSUB)
        outs.append(pltpu.make_async_copy(out_v.at[rows], out_atm.at[rows], sem.at[4 + g]))
        outs[-1].start()
    for i, (src, dst) in enumerate(((ocean_v, out_ocean), (surf_v, out_surf))):
        copies[2 + i].wait()
        outs.append(pltpu.make_async_copy(src, dst, sem.at[6 + i]))
        outs[-1].start()
    for copy in outs:
        copy.wait()


def local(n_atm, n_ocn, atm_state, level_diffusion, level_wind, vertical_rate, convective_rate,
          ocean_skin, trigger, group_order, ocean_state, ocean_neighbors, flux_sources,
          flux_weights, surface_sources, surface_weights):
    atm = atm_state.reshape(FIELDS, NLEV, ROWS, QS, 128).transpose(0, 1, 3, 2, 4).reshape(1008, 128)
    ocean = ocean_state.transpose(1, 0, 2).reshape(OLEV, 2, 8, 128).transpose(0, 2, 1, 3).reshape(320, 128)
    hbm = pl.BlockSpec(memory_space=pltpu.HBM)
    dma = pltpu.SemaphoreType.DMA

    def vmem(*shape, dtype=F32):
        return pltpu.VMEM(shape, dtype)

    parts = pl.pallas_call(
        functools.partial(kernel, n_atm, n_ocn),
        out_shape=(
            jax.ShapeDtypeStruct((8, 72, 128), F32),
            jax.ShapeDtypeStruct((8, 56, 128), F32),
            jax.ShapeDtypeStruct((320, 128), F32),
            jax.ShapeDtypeStruct((2, 128), F32),
        ),
        in_specs=[hbm] * 14,
        out_specs=(hbm,) * 4,
        scratch_shapes=[
            pltpu.SMEM((NLEV,), F32), pltpu.SMEM((NLEV,), F32),
            pltpu.SMEM((FIELDS,), F32), pltpu.SMEM((FIELDS,), F32),
            vmem(2, 128), vmem(2, 128, dtype=jnp.int32), vmem(2, 128, dtype=jnp.int32),
            vmem(4, 256, dtype=jnp.int32), vmem(4, 256),
            vmem(2, 1008, 128), vmem(13, QS, 40, 128), vmem(13, QS, 40, 128), vmem(4, 40, 128),
            *[vmem(8, 72, 128)] * 5, *[vmem(8, 56, 128)] * 5,
            vmem(LEV, 8, 128), vmem(LEV, 8, 128),
            vmem(320, 128),
            vmem(NBR, 1536, dtype=jnp.int32), vmem(NW, 1536, dtype=jnp.int32), vmem(NW, 1536),
            vmem(NT * OROW, 128), vmem(NT, PARTS * OROW, 128, dtype=BF16),
            vmem(NT - 2, 384, 128, dtype=BF16), vmem(NT * OROW, 128), vmem(16, 128),
            vmem(320, 128), vmem(2, 128),
            vmem(8, 128), vmem(8, 128), vmem(8, 128),
            dma((14,)), dma((2,)), dma((2,)), dma((8,)), dma((8,)),
            dma((2, 8)), dma((2, 8)), dma((2, 8)), dma((2, 8)), dma((2, 8)), dma((2, 8)), dma((4,)),
            dma((2,)), dma((2,)), dma((2,)),
        ],
        compiler_params=pltpu.CompilerParams(
            collective_id=0, has_side_effects=True, vmem_limit_bytes=60 * 1024 * 1024
        ),
    )(
        atm, level_diffusion, level_wind, vertical_rate, convective_rate,
        ocean_skin.reshape(2, 128), trigger.reshape(2, 128), group_order.reshape(2, 128),
        ocean, ocean_neighbors, flux_sources, flux_weights, surface_sources, surface_weights,
    )
    new_atm, new_ocean, surf = pl.pallas_call(
        finish,
        out_shape=(
            jax.ShapeDtypeStruct((1008, 128), F32),
            jax.ShapeDtypeStruct((320, 128), F32),
            jax.ShapeDtypeStruct((2, 128), F32),
        ),
        in_specs=[hbm] * 4,
        out_specs=(hbm,) * 3,
        scratch_shapes=[
            vmem(8, 72, 128), vmem(8, 56, 128), vmem(320, 128), vmem(2, 128), vmem(1008, 128), dma((8,)),
        ],
        compiler_params=pltpu.CompilerParams(vmem_limit_bytes=60 * 1024 * 1024),
    )(*parts)
    new_atm = new_atm.reshape(FIELDS, NLEV, QS, ROWS, 128).transpose(0, 1, 3, 2, 4)
    new_ocean = new_ocean.reshape(OLEV, 8, 2, 128).transpose(0, 2, 1, 3).reshape(OLEV, 2, 1024)
    return (
        new_atm.reshape(FIELDS, NLEV, ROWS, QS * 128),
        new_ocean.transpose(1, 0, 2),
        surf.reshape(256),
    )


def solution(mesh):
    both = ("atm", "ocn")
    return jax.shard_map(
        functools.partial(local, mesh.shape["atm"], mesh.shape["ocn"]),
        mesh=mesh,
        in_specs=(
            P(None, "ocn", "atm", None), P("ocn"), P("ocn"), P(), P(),
            P(both), P(both), P(both), P(None, None, both),
            P(None, both), P(None, both), P(None, both), P(None, both), P(None, both),
        ),
        out_specs=(P(None, "ocn", "atm", None), P(None, None, both), P(both)),
        check_vma=False,
    )
```

```python
import functools

import jax
import jax.numpy as jnp
from jax import lax
from jax.experimental import pallas as pl
from jax.experimental.pallas import tpu as pltpu
from jax.sharding import PartitionSpec as P

MESH = pl.DeviceIdType.MESH
F32 = jnp.float32
BF16 = jnp.bfloat16

FIELDS = 7
LEV = 72
NLEV = 9
ROWS = 4
QS = 4
DYN_STEPS = 4
PHYS_ITERS = 3
CONV_ITERS = 24
OLEV = 20
OSTEPS = 4
NBR = 6
NW = 4
PARTS = 3
OROW = 48
NT = 12
OCEAN_SPREAD = 0.6
OCEAN_VERTICAL = 0.2
HEAT_COEF = 0.5
MOIST_COEF = 0.5
HEAT_BACK = 0.3
MOIST_BACK = 0.3
OCEAN_FORCE = 0.3

GROUPS = ((0, 4), (4, 3))
HSUB = 16


def iota(shape, dim):
    return lax.broadcasted_iota(jnp.int32, shape, dim)


def kernel(
    n_atm,
    n_ocn,
    atm, ld, lw, vr, cr, skin, trig, order, ocean, nbr, fsrc, fw, ssrc, sw,
    ba0, ba1, out_ocean, out_surf,
    ld_s, lw_s, vr_s, cr_s, skin_v, trig_v, order_v, ssrc_v, sw_v,
    nb, dd, coef,
    sa0, ra0, sc0, rc0, pa0, sa1, ra1, sc1, rc1, pa1,
    xa, xb,
    oc_o, nbr_e, fsrc_e, fw_e,
    st, hs, mm, ff, uu, oout, sout,
    fl, fl_l, fl_r,
    local_sem, halo_send, halo_recv, oh_send, oh_recv,
    a_send, a_recv, b_send, b_recv, c_send, c_recv, self_sem, f_send, f_recv, out_sem,
):
    a = lax.axis_index("atm")
    o = lax.axis_index("ocn")
    dev = a * n_ocn + o
    odd = lax.rem(a, 2)
    mate = a + 1 - 2 * odd
    cross = lax.rem(a + n_atm - 1 + 2 * odd, n_atm)
    total = n_atm * n_ocn
    left = lax.rem(dev + total - 1, total)
    right = lax.rem(dev + 1, total)
    left_id = (left // n_ocn, lax.rem(left, n_ocn))
    right_id = (right // n_ocn, lax.rem(right, n_ocn))
    def at_offset(dx, dy):
        return lax.rem(o // 2 + dx, n_ocn // 2) * 2 + lax.rem(o + dy, 2)

    peers = [at_offset(*d) for d in ((2, 1), (1, 1), (3, 1), (2, 0), (1, 0), (3, 0), (0, 1))]
    others = [at_offset(*d) for d in ((2, 0), (1, 0), (3, 0), (2, 1), (0, 0), (1, 1), (3, 1), (0, 1))]

    fills = [
        (ld, ld_s), (lw, lw_s), (vr, vr_s), (cr, cr_s),
        (skin, skin_v), (trig, trig_v), (order, order_v), (ssrc, ssrc_v), (sw, sw_v),
        (atm, nb.at[0]), (ocean, oc_o),
        (nbr, nbr_e.at[:, pl.ds(256, 1024)]),
        (fsrc, fsrc_e.at[:, pl.ds(256, 1024)]),
        (fw, fw_e.at[:, pl.ds(256, 1024)]),
    ]
    fills = [
        pltpu.make_async_copy(src, dst, local_sem.at[i]) for i, (src, dst) in enumerate(fills)
    ]
    for copy in fills:
        copy.start()

    edge_row = jnp.where(odd == 1, n_atm - 1, 0)
    inside = a != edge_row
    keep = jnp.where(inside, 1.0, 0.0).astype(F32)
    barrier = pltpu.get_barrier_semaphore()
    partners = [(mate, o), left_id, right_id] + [(a, p) for p in peers]

    def greet(devices):
        for device in devices:
            pl.semaphore_signal(barrier, inc=1, device_id=device, device_id_type=MESH)

    greet(partners)

    @pl.when(inside)
    def _():
        greet([(cross, p) for p in others])

    def remote(src, dst, send, recv, device):
        return pltpu.make_async_remote_copy(
            src_ref=src, dst_ref=dst, send_sem=send, recv_sem=recv,
            device_id=device, device_id_type=MESH,
        )

    for copy in fills:
        copy.wait()

    sends = (sa0, sa1)
    takes = (ra0, ra1)
    gives = (sc0, sc1)
    adds = (rc0, rc1)
    packs = (pa0, pa1)
    backs = (ba0, ba1)

    def enter(g, b):
        f0, nf = GROUPS[g]
        n = nf * NLEV
        for q in range(QS):
            block = [
                nb[b, pl.ds(f0 * NLEV * HSUB + 4 * q + r, n, stride=HSUB), :] for r in range(ROWS)
            ]
            for r in range(ROWS):
                piece = jnp.where(odd == 1, block[ROWS - 1 - r], block[r])
                dd[g, 0, 1 + (b + 1) * ROWS + r, q, pl.ds(0, n), :] = piece

    def update(g, step, i):
        n = GROUPS[g][1] * NLEV
        rows = pl.ds(0, n)
        lane = iota((n, 128), 1)
        here = [dd[g, step - 1, i, q, rows, :] for q in range(QS)]
        to_east = [pltpu.roll(x, 1, 1) for x in here]
        to_west = [pltpu.roll(x, 127, 1) for x in here]
        new = []
        for q in range(QS):
            west = jnp.where(lane == 0, to_east[(q - 1) % QS], to_east[q])
            east = jnp.where(lane == 127, to_west[(q + 1) % QS], to_west[q])
            beside = dd[g, step - 1, i - 1, q, rows, :] + dd[g, step - 1, i + 1, q, rows, :]
            new.append(
                coef[g, 0, rows, :] * here[q]
                + coef[g, 1, rows, :] * beside
                + coef[g, 2, rows, :] * east
                + coef[g, 3, rows, :] * west
            )
        return new

    def steps(g, first, dst):
        n = GROUPS[g][1] * NLEV

        def scaled(i, value):
            return value * jnp.where(i <= ROWS, keep, 1.0) if first <= ROWS else value

        for step in range(1, DYN_STEPS):

            def row(i, carry):
                for q, value in enumerate(update(g, step, i)):
                    dd[g, step, i, q, pl.ds(0, n), :] = scaled(i, value)
                return carry

            begin = first + DYN_STEPS - step
            lax.fori_loop(begin, begin + ROWS, row, 0, unroll=True)

        def last(i, carry):
            r = jnp.where(odd == 1, ROWS - 1 - i, i)
            for q, value in enumerate(update(g, DYN_STEPS, i + first)):
                dst[r * 2 + q // 2, pl.ds((q % 2) * n, n), :] = scaled(i + first, value)
            return carry

        lax.fori_loop(0, ROWS, last, 0, unroll=True)

    def contribute(g):
        n = GROUPS[g][1] * NLEV
        sub = lax.rem(iota((n, 128), 0), NLEV)
        diff = jnp.zeros((n, 128), F32)
        wind = jnp.zeros((n, 128), F32)
        for l in range(NLEV):
            diff = jnp.where(sub == l, ld_s[l], diff)
            wind = jnp.where(sub == l, lw_s[l], wind)
        coef[g, 0, pl.ds(0, n), :] = 1.0 - 4.0 * diff
        coef[g, 1, pl.ds(0, n), :] = diff
        coef[g, 2, pl.ds(0, n), :] = diff - 0.5 * wind
        coef[g, 3, pl.ds(0, n), :] = diff + 0.5 * wind
        none = jnp.zeros((n, 128), F32)
        for step in range(DYN_STEPS):
            for q in range(QS):
                for i in (ROWS - 1 - step, ROWS - step):
                    dd[g, step, i, q, pl.ds(0, n), :] = none
        enter(g, 0)
        steps(g, 1, gives[g])

    def send_across(g):
        copies = [
            remote(gives[g].at[p], adds[g].at[o], c_send.at[g, p], c_recv.at[g, o], (cross, p))
            for p in others
        ]
        arrivals = [
            remote(gives[g].at[p], adds[g].at[p], c_send.at[g, p], c_recv.at[g, p], (cross, p))
            for p in others
        ]

        @pl.when(inside)
        def _():
            for copy in copies:
                copy.start()

        @pl.when(jnp.logical_not(inside))
        def _():
            adds[g][...] = jnp.zeros(adds[g].shape, F32)

        return copies, arrivals

    contribute(0)

    @pl.when(inside)
    def _():
        pl.semaphore_wait(barrier, len(partners) + len(others))

    @pl.when(jnp.logical_not(inside))
    def _():
        pl.semaphore_wait(barrier, len(partners))

    halos = []
    for g, (f0, nf) in enumerate(GROUPS):
        rows = pl.ds(f0 * NLEV * HSUB, nf * NLEV * HSUB)
        copy = remote(atm.at[rows], nb.at[1, rows], halo_send.at[g], halo_recv.at[g], (mate, o))
        copy.start()
        halos.append(copy)

    unused = jnp.zeros((4, 128), F32)
    for u in range(2, 10):
        for f in range(2):
            piece = oc_o[pl.ds((u - 2) * 2 + f, OLEV, stride=16), :]
            st[pl.ds(u * OROW + f * 24, OLEV), :] = piece
            st[pl.ds(u * OROW + f * 24 + OLEV, 4), :] = unused

    def tiles(u):
        return st.at[pl.ds(u * OROW, 2 * OROW)]

    last, first = pl.ds(896, 128), pl.ds(0, 128)
    low, high = pl.ds(128, 128), pl.ds(1280, 128)
    edge = [
        (tiles(8), tiles(0), right_id),
        (nbr.at[:, last], nbr_e.at[:, low], right_id),
        (fsrc.at[:, last], fsrc_e.at[:, low], right_id),
        (fw.at[:, last], fw_e.at[:, low], right_id),
        (tiles(2), tiles(10), left_id),
        (nbr.at[:, first], nbr_e.at[:, high], left_id),
        (fsrc.at[:, first], fsrc_e.at[:, high], left_id),
        (fw.at[:, first], fw_e.at[:, high], left_id),
    ]
    edges = [
        remote(src, dst, oh_send.at[i], oh_recv.at[i], device)
        for i, (src, dst, device) in enumerate(edge)
    ]
    for copy in edges:
        copy.start()

    out_cross = [send_across(0)]

    def exchange(src, dst, send, recv, own_sem, g):
        copies = [
            remote(src.at[p], dst.at[o], send.at[g, p], recv.at[g, o], (a, p)) for p in peers
        ]
        own = pltpu.make_async_copy(src.at[o], dst.at[o], own_sem)
        for copy in copies:
            copy.start()
        own.start()
        arrivals = [
            remote(src.at[p], dst.at[p], send.at[g, p], recv.at[g, p], (a, p)) for p in peers
        ]
        return copies, own, arrivals

    def crossed(handle):
        @pl.when(inside)
        def _():
            for copy in handle[1]:
                copy.wait_recv()

    def landed(handle):
        copies, own, arrivals = handle
        own.wait()
        for copy in arrivals:
            copy.wait_recv()

    out_there = []
    for g in range(2):
        halos[g].wait_recv()
        enter(g, 1)
        steps(g, 1 + ROWS, sends[g])
        out_there.append(exchange(sends[g], takes[g], a_send, a_recv, self_sem.at[g], g))
        if g == 0:
            contribute(1)
            out_cross.append(send_across(1))

    hit = jnp.where(trig_v[...] > 0, order_v[...], -1).astype(F32)
    hit = jnp.concatenate([hit, jnp.full((6, 128), -1.0, F32)], axis=0)
    hit = jnp.transpose(hit, (1, 0))
    lane = iota((128, 128), 1)
    active = []
    for half in range(2):
        column = (lane + 128 * half).astype(F32)
        mark = jnp.where(hit[:, 0:1] == column, 1.0, 0.0) + jnp.where(hit[:, 1:2] == column, 1.0, 0.0)
        active.append(jnp.sum(mark, axis=0, keepdims=True))

    for copy in edges:
        copy.wait_recv()
    for copy in edges:
        copy.wait_send()

    def build(u, carry):
        at = pl.multiple_of(u * 128, 128)
        k = iota((192, 128), 0) + 96
        base = iota((1, 128), 1) + 128
        count = jnp.zeros((192, 128), F32)
        for j in range(NBR):
            target = nbr_e[pl.ds(j, 1), pl.ds(at, 128)] + base
            count = count + jnp.where(k == target, 1.0, 0.0)
        mm[u - 1, pl.ds(0, 96), :] = jnp.zeros((96, 128), BF16)
        mm[u - 1, pl.ds(96, 192), :] = count.astype(BF16)
        mm[u - 1, pl.ds(288, 96), :] = jnp.zeros((96, 128), BF16)
        return carry

    lax.fori_loop(1, NT - 1, build, 0, unroll=True)

    level_row = lax.rem(iota((OROW, 128), 0), 24)

    def spread(force):
        def split(u, carry):
            rest = st[pl.ds(pl.multiple_of(u * OROW, OROW), OROW), :]
            for part in range(PARTS):
                piece = rest.astype(BF16)
                hs[u, pl.ds(part * OROW, OROW), :] = piece
                rest = rest - piece.astype(F32)
            return carry

        lax.fori_loop(0, NT, split, 0, unroll=True)

        def tile(u, carry):
            source = jnp.concatenate([hs[u - 1], hs[u], hs[u + 1]], axis=1)
            sums = jnp.dot(source, mm[u - 1], preferred_element_type=F32)
            around = sums[0:OROW]
            for part in range(1, PARTS):
                around = around + sums[part * OROW : (part + 1) * OROW]
            rows = pl.ds(pl.multiple_of(u * OROW, OROW), OROW)
            here = st[rows, :]
            here = here + OCEAN_SPREAD * (around * (1.0 / 6.0) - here)
            above = jnp.where(level_row == 0, here, pltpu.roll(here, 1, 0))
            below = jnp.where(level_row == OLEV - 1, here, pltpu.roll(here, OROW - 1, 0))
            here = here + OCEAN_VERTICAL * (above + below - 2.0 * here)
            if force:
                here = here + ff[pl.ds(pl.multiple_of(u * OROW, OROW), OROW), :]
            st[rows, :] = jnp.where(level_row < OLEV, here, 0.0)
            return carry

        lax.fori_loop(1, NT - 1, tile, 0, unroll=True)

    spread(False)

    def physics(g):
        f0, nf = GROUPS[g]
        n = 2 * nf
        x = (xa, xb)[g]
        sub = iota((n, 128), 0)
        field = lax.rem(sub, nf)
        mix = jnp.zeros((n, 128), F32)
        rate = jnp.zeros((n, 128), F32)
        for f in range(nf):
            mix = jnp.where(field == f, vr_s[f0 + f], mix)
            rate = jnp.where(field == f, cr_s[f0 + f], rate)
        rate = rate * jnp.where(sub < nf, active[0], active[1])

        for lev in range(LEV):
            rows = pl.ds(lev % NLEV, n, stride=NLEV)
            x[lev, pl.ds(0, n), :] = takes[g][lev // NLEV, rows, :] + adds[g][lev // NLEV, rows, :]

        def vertical(i, carry):
            here = x[0, pl.ds(0, n), :]
            above = here
            for lev in range(LEV):
                below = x[lev + 1, pl.ds(0, n), :] if lev < LEV - 1 else here
                x[lev, pl.ds(0, n), :] = here + mix * (above + below - 2.0 * here)
                above, here = here, below
            return carry

        lax.fori_loop(0, PHYS_ITERS, vertical, 0)

        def convect(i, carry):
            here = x[0, pl.ds(0, n), :]
            came = jnp.zeros((n, 128), F32)
            for lev in range(LEV - 1):
                below = x[lev + 1, pl.ds(0, n), :]
                transfer = rate * jnp.tanh(below - here)
                x[lev, pl.ds(0, n), :] = here + transfer - came
                came, here = transfer, below
            x[LEV - 1, pl.ds(0, n), :] = here - came
            return carry

        lax.fori_loop(0, CONV_ITERS, convect, 0)

    def pack(g):
        nf = GROUPS[g][1]
        n = 2 * nf
        x = (xa, xb)[g]
        for lev in range(LEV):
            packs[g][lev // NLEV, pl.ds(lev % NLEV, n, stride=NLEV), :] = x[lev, pl.ds(0, n), :]

    landed(out_there[0])
    crossed(out_cross[0])
    physics(0)

    fl[...] = jnp.zeros((8, 128), F32)
    for half in range(2):
        low_row = [xa[LEV - 1, pl.ds(half * 4 + f, 1), :] for f in range(4)]
        speed = jnp.sqrt(1.0 + low_row[1] * low_row[1] + low_row[2] * low_row[2])
        heat = HEAT_COEF * speed * (low_row[0] - skin_v[pl.ds(half, 1), :])
        fresh = MOIST_COEF * speed * low_row[3]
        xa[LEV - 1, pl.ds(half * 4, 1), :] = low_row[0] - HEAT_BACK * heat
        xa[LEV - 1, pl.ds(half * 4 + 3, 1), :] = low_row[3] - MOIST_BACK * fresh
        fl[pl.ds(2 * half, 1), :] = heat
        fl[pl.ds(2 * half + 1, 1), :] = fresh
    fluxes = [
        remote(fl, fl_l, f_send.at[0], f_recv.at[0], right_id),
        remote(fl, fl_r, f_send.at[1], f_recv.at[1], left_id),
    ]
    for copy in fluxes:
        copy.start()
    pack(0)
    back_home = [exchange(packs[0], backs[0], b_send, b_recv, self_sem.at[2], 0)]
    landed(out_there[1])
    crossed(out_cross[1])
    physics(1)
    pack(1)
    back_home.append(exchange(packs[1], backs[1], b_send, b_recv, self_sem.at[3], 1))

    for copy in fluxes:
        copy.wait_recv()
    near = jnp.concatenate(
        [
            fl_l[pl.ds(2, 1), :], fl[pl.ds(0, 1), :], fl[pl.ds(2, 1), :], fl_r[pl.ds(0, 1), :],
            fl_l[pl.ds(3, 1), :], fl[pl.ds(1, 1), :], fl[pl.ds(3, 1), :], fl_r[pl.ds(1, 1), :],
        ],
        axis=0,
    )
    sub8 = iota((8, 128), 0)
    chunk = lax.rem(sub8, 4)
    ff[...] = jnp.zeros(ff.shape, F32)
    for u in range(1, NT - 1):
        at = pl.ds(u * 128, 128)
        acc = jnp.zeros((8, 128), F32)
        for link in range(NW):
            source = fsrc_e[pl.ds(link, 1), at] - (dev * 256 - 128)
            source = jnp.broadcast_to(source, (8, 128))
            picked = jnp.take_along_axis(near, source & 127, axis=1, mode="promise_in_bounds")
            picked = jnp.where((source >> 7) == chunk, picked, 0.0)
            acc = acc + fw_e[pl.ds(link, 1), at] * picked
        ff[pl.ds(u * OROW, 1), :] = OCEAN_FORCE * jnp.sum(acc[0:4], axis=0, keepdims=True)
        ff[pl.ds(u * OROW + 24, 1), :] = OCEAN_FORCE * jnp.sum(acc[4:8], axis=0, keepdims=True)
    for u in range(1, NT - 1):
        for f in range(2):
            row = pl.ds(u * OROW + 24 * f, 1)
            st[row, :] = st[row, :] + ff[row, :]

    def ocean_step(i, carry):
        spread(True)
        return carry

    lax.fori_loop(1, OSTEPS, ocean_step, 0)

    for u in range(2, 10):
        for f in range(2):
            oout[pl.ds((u - 2) * 2 + f, OLEV, stride=16), :] = st[pl.ds(u * OROW + f * 24, OLEV), :]
    ocean_copy = pltpu.make_async_copy(oout, out_ocean, out_sem.at[0])
    ocean_copy.start()

    uu[...] = jnp.zeros(uu.shape, F32)
    for u in range(1, NT - 1):
        uu[pl.ds(u, 1), :] = st[pl.ds(u * OROW, 1), :]
    top = (uu[pl.ds(0, 8), :], uu[pl.ds(8, 8), :])
    for half in range(2):
        at = pl.ds(half * 128, 128)
        acc = jnp.zeros((8, 128), F32)
        for link in range(NW):
            source = ssrc_v[pl.ds(link, 1), at] - (dev * 1024 - 256)
            source = jnp.broadcast_to(source, (8, 128))
            weight = sw_v[pl.ds(link, 1), at]
            for part in range(2):
                picked = jnp.take_along_axis(top[part], source & 127, axis=1, mode="promise_in_bounds")
                picked = jnp.where((source >> 7) == sub8 + 8 * part, picked, 0.0)
                acc = acc + weight * picked
        sout[pl.ds(half, 1), :] = jnp.sum(acc, axis=0, keepdims=True)
    surf_copy = pltpu.make_async_copy(sout, out_surf, out_sem.at[1])
    surf_copy.start()

    for handle in back_home:
        landed(handle)
    for copy in halos + fluxes:
        copy.wait_send()
    for copies, own, arrivals in out_there + back_home:
        for copy in copies:
            copy.wait_send()

    @pl.when(inside)
    def _():
        for copies, arrivals in out_cross:
            for copy in copies:
                copy.wait_send()

    ocean_copy.wait()
    surf_copy.wait()


def finish(ba0, ba1, ocean, surf, out_atm, out_ocean, out_surf, b0, b1, ocean_v, surf_v, out_v, sem):
    ins = ((ba0, b0), (ba1, b1), (ocean, ocean_v), (surf, surf_v))
    copies = [pltpu.make_async_copy(src, dst, sem.at[i]) for i, (src, dst) in enumerate(ins)]
    for copy in copies:
        copy.start()
    outs = []
    for g, (f0, nf) in enumerate(GROUPS):
        n = nf * NLEV
        copies[g].wait()
        for r in range(ROWS):
            for q in range(QS):
                piece = (b0, b1)[g][2 * r + q // 2, pl.ds((q % 2) * n, n), :]
                out_v[pl.ds(f0 * NLEV * HSUB + 4 * q + r, n, stride=HSUB), :] = piece
        rows = pl.ds(f0 * NLEV * HSUB, n * HSUB)
        outs.append(pltpu.make_async_copy(out_v.at[rows], out_atm.at[rows], sem.at[4 + g]))
        outs[-1].start()
    for i, (src, dst) in enumerate(((ocean_v, out_ocean), (surf_v, out_surf))):
        copies[2 + i].wait()
        outs.append(pltpu.make_async_copy(src, dst, sem.at[6 + i]))
        outs[-1].start()
    for copy in outs:
        copy.wait()


def local(n_atm, n_ocn, atm_state, level_diffusion, level_wind, vertical_rate, convective_rate,
          ocean_skin, trigger, group_order, ocean_state, ocean_neighbors, flux_sources,
          flux_weights, surface_sources, surface_weights):
    atm = atm_state.reshape(FIELDS, NLEV, ROWS, QS, 128).transpose(0, 1, 3, 2, 4).reshape(1008, 128)
    ocean = ocean_state.transpose(1, 0, 2).reshape(OLEV, 2, 8, 128).transpose(0, 2, 1, 3).reshape(320, 128)
    hbm = pl.BlockSpec(memory_space=pltpu.HBM)
    dma = pltpu.SemaphoreType.DMA

    def vmem(*shape, dtype=F32):
        return pltpu.VMEM(shape, dtype)

    parts = pl.pallas_call(
        functools.partial(kernel, n_atm, n_ocn),
        out_shape=(
            jax.ShapeDtypeStruct((8, 72, 128), F32),
            jax.ShapeDtypeStruct((8, 56, 128), F32),
            jax.ShapeDtypeStruct((320, 128), F32),
            jax.ShapeDtypeStruct((2, 128), F32),
        ),
        in_specs=[hbm] * 14,
        out_specs=(hbm,) * 4,
        scratch_shapes=[
            pltpu.SMEM((NLEV,), F32), pltpu.SMEM((NLEV,), F32),
            pltpu.SMEM((FIELDS,), F32), pltpu.SMEM((FIELDS,), F32),
            vmem(2, 128), vmem(2, 128, dtype=jnp.int32), vmem(2, 128, dtype=jnp.int32),
            vmem(4, 256, dtype=jnp.int32), vmem(4, 256),
            vmem(2, 1008, 128), vmem(2, DYN_STEPS, 13, QS, 40, 128), vmem(2, 4, 40, 128),
            *[vmem(8, 72, 128)] * 5, *[vmem(8, 56, 128)] * 5,
            vmem(LEV, 8, 128), vmem(LEV, 8, 128),
            vmem(320, 128),
            vmem(NBR, 1536, dtype=jnp.int32), vmem(NW, 1536, dtype=jnp.int32), vmem(NW, 1536),
            vmem(NT * OROW, 128), vmem(NT, PARTS * OROW, 128, dtype=BF16),
            vmem(NT - 2, 384, 128, dtype=BF16), vmem(NT * OROW, 128), vmem(16, 128),
            vmem(320, 128), vmem(2, 128),
            vmem(8, 128), vmem(8, 128), vmem(8, 128),
            dma((14,)), dma((2,)), dma((2,)), dma((8,)), dma((8,)),
            dma((2, 8)), dma((2, 8)), dma((2, 8)), dma((2, 8)), dma((2, 8)), dma((2, 8)), dma((4,)),
            dma((2,)), dma((2,)), dma((2,)),
        ],
        compiler_params=pltpu.CompilerParams(
            collective_id=0, has_side_effects=True, vmem_limit_bytes=60 * 1024 * 1024
        ),
    )(
        atm, level_diffusion, level_wind, vertical_rate, convective_rate,
        ocean_skin.reshape(2, 128), trigger.reshape(2, 128), group_order.reshape(2, 128),
        ocean, ocean_neighbors, flux_sources, flux_weights, surface_sources, surface_weights,
    )
    new_atm, new_ocean, surf = pl.pallas_call(
        finish,
        out_shape=(
            jax.ShapeDtypeStruct((1008, 128), F32),
            jax.ShapeDtypeStruct((320, 128), F32),
            jax.ShapeDtypeStruct((2, 128), F32),
        ),
        in_specs=[hbm] * 4,
        out_specs=(hbm,) * 3,
        scratch_shapes=[
            vmem(8, 72, 128), vmem(8, 56, 128), vmem(320, 128), vmem(2, 128), vmem(1008, 128), dma((8,)),
        ],
        compiler_params=pltpu.CompilerParams(vmem_limit_bytes=60 * 1024 * 1024),
    )(*parts)
    new_atm = new_atm.reshape(FIELDS, NLEV, QS, ROWS, 128).transpose(0, 1, 3, 2, 4)
    new_ocean = new_ocean.reshape(OLEV, 8, 2, 128).transpose(0, 2, 1, 3).reshape(OLEV, 2, 1024)
    return (
        new_atm.reshape(FIELDS, NLEV, ROWS, QS * 128),
        new_ocean.transpose(1, 0, 2),
        surf.reshape(256),
    )


def solution(mesh):
    both = ("atm", "ocn")
    return jax.shard_map(
        functools.partial(local, mesh.shape["atm"], mesh.shape["ocn"]),
        mesh=mesh,
        in_specs=(
            P(None, "ocn", "atm", None), P("ocn"), P("ocn"), P(), P(),
            P(both), P(both), P(both), P(None, None, both),
            P(None, both), P(None, both), P(None, both), P(None, both), P(None, both),
        ),
        out_specs=(P(None, "ocn", "atm", None), P(None, None, both), P(both)),
        check_vma=False,
    )
```

```python
import functools

import jax
import jax.numpy as jnp
from jax import lax
from jax.experimental import pallas as pl
from jax.experimental.pallas import tpu as pltpu
from jax.sharding import PartitionSpec as P

MESH = pl.DeviceIdType.MESH
F32 = jnp.float32
BF16 = jnp.bfloat16

FIELDS = 7
LEV = 72
NLEV = 9
ROWS = 4
QS = 4
DYN_STEPS = 4
PHYS_ITERS = 3
CONV_ITERS = 24
OLEV = 20
OSTEPS = 4
NBR = 6
NW = 4
PARTS = 3
OROW = 48
NT = 12
OCEAN_SPREAD = 0.6
OCEAN_VERTICAL = 0.2
HEAT_COEF = 0.5
MOIST_COEF = 0.5
HEAT_BACK = 0.3
MOIST_BACK = 0.3
OCEAN_FORCE = 0.3

GROUPS = ((0, 4), (4, 3))
HSUB = 16


def iota(shape, dim):
    return lax.broadcasted_iota(jnp.int32, shape, dim)


def kernel(
    n_atm,
    n_ocn,
    atm, ld, lw, vr, cr, skin, trig, order, ocean, nbr, fsrc, fw, ssrc, sw,
    ba0, ba1, out_ocean, out_surf,
    ld_s, lw_s, vr_s, cr_s, skin_v, trig_v, order_v, ssrc_v, sw_v,
    nb, dd, coef,
    sa0, ra0, sc0, rc0, pa0, sa1, ra1, sc1, rc1, pa1,
    xa, xb,
    oc_o, nbr_e, fsrc_e, fw_e,
    st, hs, mm, ff, uu, oout, sout,
    fl, fl_l, fl_r,
    local_sem, halo_send, halo_recv, oh_send, oh_recv,
    a_send, a_recv, b_send, b_recv, c_send, c_recv, self_sem, f_send, f_recv, out_sem,
):
    a = lax.axis_index("atm")
    o = lax.axis_index("ocn")
    dev = a * n_ocn + o
    odd = lax.rem(a, 2)
    mate = a + 1 - 2 * odd
    cross = lax.rem(a + n_atm - 1 + 2 * odd, n_atm)
    total = n_atm * n_ocn
    left = lax.rem(dev + total - 1, total)
    right = lax.rem(dev + 1, total)
    left_id = (left // n_ocn, lax.rem(left, n_ocn))
    right_id = (right // n_ocn, lax.rem(right, n_ocn))
    def at_offset(dx, dy):
        return lax.rem(o // 2 + dx, n_ocn // 2) * 2 + lax.rem(o + dy, 2)

    peers = [at_offset(*d) for d in ((2, 1), (1, 1), (3, 1), (2, 0), (1, 0), (3, 0), (0, 1))]
    others = [at_offset(*d) for d in ((2, 0), (1, 0), (3, 0), (2, 1), (0, 0), (1, 1), (3, 1), (0, 1))]

    fills = [
        (ld, ld_s), (lw, lw_s), (vr, vr_s), (cr, cr_s),
        (skin, skin_v), (trig, trig_v), (order, order_v), (ssrc, ssrc_v), (sw, sw_v),
        (atm, nb.at[0]), (ocean, oc_o),
        (nbr, nbr_e.at[:, pl.ds(256, 1024)]),
        (fsrc, fsrc_e.at[:, pl.ds(256, 1024)]),
        (fw, fw_e.at[:, pl.ds(256, 1024)]),
    ]
    fills = [
        pltpu.make_async_copy(src, dst, local_sem.at[i]) for i, (src, dst) in enumerate(fills)
    ]
    for copy in fills:
        copy.start()

    edge_row = jnp.where(odd == 1, n_atm - 1, 0)
    inside = a != edge_row
    keep = jnp.where(inside, 1.0, 0.0).astype(F32)
    barrier = pltpu.get_barrier_semaphore()
    partners = [(mate, o), left_id, right_id] + [(a, p) for p in peers]

    def greet(devices):
        for device in devices:
            pl.semaphore_signal(barrier, inc=1, device_id=device, device_id_type=MESH)

    greet(partners)

    @pl.when(inside)
    def _():
        greet([(cross, p) for p in others])

    def remote(src, dst, send, recv, device):
        return pltpu.make_async_remote_copy(
            src_ref=src, dst_ref=dst, send_sem=send, recv_sem=recv,
            device_id=device, device_id_type=MESH,
        )

    for copy in fills:
        copy.wait()

    sends = (sa0, sa1)
    takes = (ra0, ra1)
    gives = (sc0, sc1)
    adds = (rc0, rc1)
    packs = (pa0, pa1)
    backs = (ba0, ba1)

    def enter(g, b):
        f0, nf = GROUPS[g]
        n = nf * NLEV
        for q in range(QS):
            block = [
                nb[b, pl.ds(f0 * NLEV * HSUB + 4 * q + r, n, stride=HSUB), :] for r in range(ROWS)
            ]
            for r in range(ROWS):
                piece = jnp.where(odd == 1, block[ROWS - 1 - r], block[r])
                dd[g, 0, 1 + (b + 1) * ROWS + r, q, pl.ds(0, n), :] = piece

    def update(g, step, i):
        n = GROUPS[g][1] * NLEV
        rows = pl.ds(0, n)
        lane = iota((n, 128), 1)
        here = [dd[g, step - 1, i, q, rows, :] for q in range(QS)]
        to_east = [pltpu.roll(x, 1, 1) for x in here]
        to_west = [pltpu.roll(x, 127, 1) for x in here]
        new = []
        for q in range(QS):
            west = jnp.where(lane == 0, to_east[(q - 1) % QS], to_east[q])
            east = jnp.where(lane == 127, to_west[(q + 1) % QS], to_west[q])
            beside = dd[g, step - 1, i - 1, q, rows, :] + dd[g, step - 1, i + 1, q, rows, :]
            new.append(
                coef[g, 0, rows, :] * here[q]
                + coef[g, 1, rows, :] * beside
                + coef[g, 2, rows, :] * east
                + coef[g, 3, rows, :] * west
            )
        return new

    def steps(g, first, dst):
        n = GROUPS[g][1] * NLEV

        def scaled(i, value):
            return value * jnp.where(i <= ROWS, keep, 1.0) if first <= ROWS else value

        for step in range(1, DYN_STEPS):

            def row(i, carry):
                for q, value in enumerate(update(g, step, i)):
                    dd[g, step, i, q, pl.ds(0, n), :] = scaled(i, value)
                return carry

            begin = first + DYN_STEPS - step
            lax.fori_loop(begin, begin + ROWS, row, 0, unroll=True)

        def last(i, carry):
            r = jnp.where(odd == 1, ROWS - 1 - i, i)
            for q, value in enumerate(update(g, DYN_STEPS, i + first)):
                dst[r * 2 + q // 2, pl.ds((q % 2) * n, n), :] = scaled(i + first, value)
            return carry

        lax.fori_loop(0, ROWS, last, 0, unroll=True)

    def contribute(g):
        n = GROUPS[g][1] * NLEV
        sub = lax.rem(iota((n, 128), 0), NLEV)
        diff = jnp.zeros((n, 128), F32)
        wind = jnp.zeros((n, 128), F32)
        for l in range(NLEV):
            diff = jnp.where(sub == l, ld_s[l], diff)
            wind = jnp.where(sub == l, lw_s[l], wind)
        coef[g, 0, pl.ds(0, n), :] = 1.0 - 4.0 * diff
        coef[g, 1, pl.ds(0, n), :] = diff
        coef[g, 2, pl.ds(0, n), :] = diff - 0.5 * wind
        coef[g, 3, pl.ds(0, n), :] = diff + 0.5 * wind
        none = jnp.zeros((n, 128), F32)
        for step in range(DYN_STEPS):
            for q in range(QS):
                for i in (ROWS - 1 - step, ROWS - step):
                    dd[g, step, i, q, pl.ds(0, n), :] = none
        enter(g, 0)
        steps(g, 1, gives[g])

    def send_across(g):
        copies = [
            remote(gives[g].at[p], adds[g].at[o], c_send.at[g], c_recv.at[g], (cross, p))
            for p in others
        ]
        whole = remote(gives[g], adds[g], c_send.at[g], c_recv.at[g], (cross, o))

        @pl.when(inside)
        def _():
            for copy in copies:
                copy.start()

        @pl.when(jnp.logical_not(inside))
        def _():
            adds[g][...] = jnp.zeros(adds[g].shape, F32)

        return whole

    contribute(0)

    @pl.when(inside)
    def _():
        pl.semaphore_wait(barrier, len(partners) + len(others))

    @pl.when(jnp.logical_not(inside))
    def _():
        pl.semaphore_wait(barrier, len(partners))

    halos = []
    for g, (f0, nf) in enumerate(GROUPS):
        rows = pl.ds(f0 * NLEV * HSUB, nf * NLEV * HSUB)
        copy = remote(atm.at[rows], nb.at[1, rows], halo_send.at[g], halo_recv.at[g], (mate, o))
        copy.start()
        halos.append(copy)

    unused = jnp.zeros((4, 128), F32)
    for u in range(2, 10):
        for f in range(2):
            piece = oc_o[pl.ds((u - 2) * 2 + f, OLEV, stride=16), :]
            st[pl.ds(u * OROW + f * 24, OLEV), :] = piece
            st[pl.ds(u * OROW + f * 24 + OLEV, 4), :] = unused

    def tiles(u):
        return st.at[pl.ds(u * OROW, 2 * OROW)]

    last, first = pl.ds(896, 128), pl.ds(0, 128)
    low, high = pl.ds(128, 128), pl.ds(1280, 128)
    edge = [
        (tiles(8), tiles(0), right_id),
        (nbr.at[:, last], nbr_e.at[:, low], right_id),
        (fsrc.at[:, last], fsrc_e.at[:, low], right_id),
        (fw.at[:, last], fw_e.at[:, low], right_id),
        (tiles(2), tiles(10), left_id),
        (nbr.at[:, first], nbr_e.at[:, high], left_id),
        (fsrc.at[:, first], fsrc_e.at[:, high], left_id),
        (fw.at[:, first], fw_e.at[:, high], left_id),
    ]
    edges = [
        remote(src, dst, oh_send.at[i], oh_recv.at[i], device)
        for i, (src, dst, device) in enumerate(edge)
    ]
    for copy in edges:
        copy.start()

    out_cross = [send_across(0)]

    def exchange(src, dst, send, recv, own_sem, g):
        copies = [
            remote(src.at[p], dst.at[o], send.at[g], recv.at[g], (a, p)) for p in peers
        ]
        own = pltpu.make_async_copy(src.at[o], dst.at[o], own_sem)
        for copy in copies:
            copy.start()
        own.start()
        seven = pl.ds(0, n_ocn - 1)
        return remote(src.at[seven], dst.at[seven], send.at[g], recv.at[g], (a, peers[0])), own

    def crossed(handle):
        @pl.when(inside)
        def _():
            handle.wait_recv()

    def landed(handle):
        whole, own = handle
        own.wait()
        whole.wait_recv()

    out_there = []
    for g in range(2):
        halos[g].wait_recv()
        enter(g, 1)
        steps(g, 1 + ROWS, sends[g])
        out_there.append(exchange(sends[g], takes[g], a_send, a_recv, self_sem.at[g], g))
        if g == 0:
            contribute(1)
            out_cross.append(send_across(1))

    hit = jnp.where(trig_v[...] > 0, order_v[...], -1).astype(F32)
    hit = jnp.concatenate([hit, jnp.full((6, 128), -1.0, F32)], axis=0)
    hit = jnp.transpose(hit, (1, 0))
    lane = iota((128, 128), 1)
    active = []
    for half in range(2):
        column = (lane + 128 * half).astype(F32)
        mark = jnp.where(hit[:, 0:1] == column, 1.0, 0.0) + jnp.where(hit[:, 1:2] == column, 1.0, 0.0)
        active.append(jnp.sum(mark, axis=0, keepdims=True))

    for copy in edges:
        copy.wait_recv()
    for copy in edges:
        copy.wait_send()

    def build(u, carry):
        at = pl.multiple_of(u * 128, 128)
        k = iota((192, 128), 0) + 96
        base = iota((1, 128), 1) + 128
        count = jnp.zeros((192, 128), F32)
        for j in range(NBR):
            target = nbr_e[pl.ds(j, 1), pl.ds(at, 128)] + base
            count = count + jnp.where(k == target, 1.0, 0.0)
        mm[u - 1, pl.ds(0, 96), :] = jnp.zeros((96, 128), BF16)
        mm[u - 1, pl.ds(96, 192), :] = count.astype(BF16)
        mm[u - 1, pl.ds(288, 96), :] = jnp.zeros((96, 128), BF16)
        return carry

    lax.fori_loop(1, NT - 1, build, 0, unroll=True)

    level_row = lax.rem(iota((OROW, 128), 0), 24)

    def spread(force):
        def split(u, carry):
            rest = st[pl.ds(pl.multiple_of(u * OROW, OROW), OROW), :]
            for part in range(PARTS):
                piece = rest.astype(BF16)
                hs[u, pl.ds(part * OROW, OROW), :] = piece
                rest = rest - piece.astype(F32)
            return carry

        lax.fori_loop(0, NT, split, 0, unroll=True)

        def tile(u, carry):
            source = jnp.concatenate([hs[u - 1], hs[u], hs[u + 1]], axis=1)
            sums = jnp.dot(source, mm[u - 1], preferred_element_type=F32)
            around = sums[0:OROW]
            for part in range(1, PARTS):
                around = around + sums[part * OROW : (part + 1) * OROW]
            rows = pl.ds(pl.multiple_of(u * OROW, OROW), OROW)
            here = st[rows, :]
            here = here + OCEAN_SPREAD * (around * (1.0 / 6.0) - here)
            above = jnp.where(level_row == 0, here, pltpu.roll(here, 1, 0))
            below = jnp.where(level_row == OLEV - 1, here, pltpu.roll(here, OROW - 1, 0))
            here = here + OCEAN_VERTICAL * (above + below - 2.0 * here)
            if force:
                here = here + ff[pl.ds(pl.multiple_of(u * OROW, OROW), OROW), :]
            st[rows, :] = jnp.where(level_row < OLEV, here, 0.0)
            return carry

        lax.fori_loop(1, NT - 1, tile, 0, unroll=True)

    spread(False)

    def physics(g):
        f0, nf = GROUPS[g]
        n = 2 * nf
        x = (xa, xb)[g]
        sub = iota((n, 128), 0)
        field = lax.rem(sub, nf)
        mix = jnp.zeros((n, 128), F32)
        rate = jnp.zeros((n, 128), F32)
        for f in range(nf):
            mix = jnp.where(field == f, vr_s[f0 + f], mix)
            rate = jnp.where(field == f, cr_s[f0 + f], rate)
        rate = rate * jnp.where(sub < nf, active[0], active[1])

        for lev in range(LEV):
            rows = pl.ds(lev % NLEV, n, stride=NLEV)
            x[lev, pl.ds(0, n), :] = takes[g][lev // NLEV, rows, :] + adds[g][lev // NLEV, rows, :]

        def vertical(i, carry):
            here = x[0, pl.ds(0, n), :]
            above = here
            for lev in range(LEV):
                below = x[lev + 1, pl.ds(0, n), :] if lev < LEV - 1 else here
                x[lev, pl.ds(0, n), :] = here + mix * (above + below - 2.0 * here)
                above, here = here, below
            return carry

        lax.fori_loop(0, PHYS_ITERS, vertical, 0)

        def convect(i, carry):
            here = x[0, pl.ds(0, n), :]
            came = jnp.zeros((n, 128), F32)
            for lev in range(LEV - 1):
                below = x[lev + 1, pl.ds(0, n), :]
                transfer = rate * jnp.tanh(below - here)
                x[lev, pl.ds(0, n), :] = here + transfer - came
                came, here = transfer, below
            x[LEV - 1, pl.ds(0, n), :] = here - came
            return carry

        lax.fori_loop(0, CONV_ITERS, convect, 0)

    def pack(g):
        nf = GROUPS[g][1]
        n = 2 * nf
        x = (xa, xb)[g]
        for lev in range(LEV):
            packs[g][lev // NLEV, pl.ds(lev % NLEV, n, stride=NLEV), :] = x[lev, pl.ds(0, n), :]

    landed(out_there[0])
    crossed(out_cross[0])
    physics(0)

    fl[...] = jnp.zeros((8, 128), F32)
    for half in range(2):
        low_row = [xa[LEV - 1, pl.ds(half * 4 + f, 1), :] for f in range(4)]
        speed = jnp.sqrt(1.0 + low_row[1] * low_row[1] + low_row[2] * low_row[2])
        heat = HEAT_COEF * speed * (low_row[0] - skin_v[pl.ds(half, 1), :])
        fresh = MOIST_COEF * speed * low_row[3]
        xa[LEV - 1, pl.ds(half * 4, 1), :] = low_row[0] - HEAT_BACK * heat
        xa[LEV - 1, pl.ds(half * 4 + 3, 1), :] = low_row[3] - MOIST_BACK * fresh
        fl[pl.ds(2 * half, 1), :] = heat
        fl[pl.ds(2 * half + 1, 1), :] = fresh
    fluxes = [
        remote(fl, fl_l, f_send.at[0], f_recv.at[0], right_id),
        remote(fl, fl_r, f_send.at[1], f_recv.at[1], left_id),
    ]
    for copy in fluxes:
        copy.start()
    pack(0)
    back_home = [exchange(packs[0], backs[0], b_send, b_recv, self_sem.at[2], 0)]
    landed(out_there[1])
    crossed(out_cross[1])
    physics(1)
    pack(1)
    back_home.append(exchange(packs[1], backs[1], b_send, b_recv, self_sem.at[3], 1))

    for copy in fluxes:
        copy.wait_recv()
    near = jnp.concatenate(
        [
            fl_l[pl.ds(2, 1), :], fl[pl.ds(0, 1), :], fl[pl.ds(2, 1), :], fl_r[pl.ds(0, 1), :],
            fl_l[pl.ds(3, 1), :], fl[pl.ds(1, 1), :], fl[pl.ds(3, 1), :], fl_r[pl.ds(1, 1), :],
        ],
        axis=0,
    )
    sub8 = iota((8, 128), 0)
    chunk = lax.rem(sub8, 4)
    ff[...] = jnp.zeros(ff.shape, F32)
    for u in range(1, NT - 1):
        at = pl.ds(u * 128, 128)
        acc = jnp.zeros((8, 128), F32)
        for link in range(NW):
            source = fsrc_e[pl.ds(link, 1), at] - (dev * 256 - 128)
            source = jnp.broadcast_to(source, (8, 128))
            picked = jnp.take_along_axis(near, source & 127, axis=1, mode="promise_in_bounds")
            picked = jnp.where((source >> 7) == chunk, picked, 0.0)
            acc = acc + fw_e[pl.ds(link, 1), at] * picked
        ff[pl.ds(u * OROW, 1), :] = OCEAN_FORCE * jnp.sum(acc[0:4], axis=0, keepdims=True)
        ff[pl.ds(u * OROW + 24, 1), :] = OCEAN_FORCE * jnp.sum(acc[4:8], axis=0, keepdims=True)
    for u in range(1, NT - 1):
        for f in range(2):
            row = pl.ds(u * OROW + 24 * f, 1)
            st[row, :] = st[row, :] + ff[row, :]

    def ocean_step(i, carry):
        spread(True)
        return carry

    lax.fori_loop(1, OSTEPS, ocean_step, 0)

    for u in range(2, 10):
        for f in range(2):
            oout[pl.ds((u - 2) * 2 + f, OLEV, stride=16), :] = st[pl.ds(u * OROW + f * 24, OLEV), :]
    ocean_copy = pltpu.make_async_copy(oout, out_ocean, out_sem.at[0])
    ocean_copy.start()

    uu[...] = jnp.zeros(uu.shape, F32)
    for u in range(1, NT - 1):
        uu[pl.ds(u, 1), :] = st[pl.ds(u * OROW, 1), :]
    top = (uu[pl.ds(0, 8), :], uu[pl.ds(8, 8), :])
    for half in range(2):
        at = pl.ds(half * 128, 128)
        acc = jnp.zeros((8, 128), F32)
        for link in range(NW):
            source = ssrc_v[pl.ds(link, 1), at] - (dev * 1024 - 256)
            source = jnp.broadcast_to(source, (8, 128))
            weight = sw_v[pl.ds(link, 1), at]
            for part in range(2):
                picked = jnp.take_along_axis(top[part], source & 127, axis=1, mode="promise_in_bounds")
                picked = jnp.where((source >> 7) == sub8 + 8 * part, picked, 0.0)
                acc = acc + weight * picked
        sout[pl.ds(half, 1), :] = jnp.sum(acc, axis=0, keepdims=True)
    surf_copy = pltpu.make_async_copy(sout, out_surf, out_sem.at[1])
    surf_copy.start()

    for copy in halos + fluxes:
        copy.wait_send()
    for whole, own in out_there:
        whole.wait_send()

    @pl.when(inside)
    def _():
        for whole in out_cross:
            whole.wait_send()

    for whole, own in back_home:
        whole.wait_send()
    for handle in back_home:
        landed(handle)
    ocean_copy.wait()
    surf_copy.wait()


def finish(ba0, ba1, ocean, surf, out_atm, out_ocean, out_surf, b0, b1, ocean_v, surf_v, out_v, sem):
    ins = ((ba0, b0), (ba1, b1), (ocean, ocean_v), (surf, surf_v))
    copies = [pltpu.make_async_copy(src, dst, sem.at[i]) for i, (src, dst) in enumerate(ins)]
    for copy in copies:
        copy.start()
    outs = []
    for g, (f0, nf) in enumerate(GROUPS):
        n = nf * NLEV
        copies[g].wait()
        for r in range(ROWS):
            for q in range(QS):
                piece = (b0, b1)[g][2 * r + q // 2, pl.ds((q % 2) * n, n), :]
                out_v[pl.ds(f0 * NLEV * HSUB + 4 * q + r, n, stride=HSUB), :] = piece
        rows = pl.ds(f0 * NLEV * HSUB, n * HSUB)
        outs.append(pltpu.make_async_copy(out_v.at[rows], out_atm.at[rows], sem.at[4 + g]))
        outs[-1].start()
    for i, (src, dst) in enumerate(((ocean_v, out_ocean), (surf_v, out_surf))):
        copies[2 + i].wait()
        outs.append(pltpu.make_async_copy(src, dst, sem.at[6 + i]))
        outs[-1].start()
    for copy in outs:
        copy.wait()


def local(n_atm, n_ocn, atm_state, level_diffusion, level_wind, vertical_rate, convective_rate,
          ocean_skin, trigger, group_order, ocean_state, ocean_neighbors, flux_sources,
          flux_weights, surface_sources, surface_weights):
    atm = atm_state.reshape(FIELDS, NLEV, ROWS, QS, 128).transpose(0, 1, 3, 2, 4).reshape(1008, 128)
    ocean = ocean_state.transpose(1, 0, 2).reshape(OLEV, 2, 8, 128).transpose(0, 2, 1, 3).reshape(320, 128)
    hbm = pl.BlockSpec(memory_space=pltpu.HBM)
    dma = pltpu.SemaphoreType.DMA

    def vmem(*shape, dtype=F32):
        return pltpu.VMEM(shape, dtype)

    parts = pl.pallas_call(
        functools.partial(kernel, n_atm, n_ocn),
        out_shape=(
            jax.ShapeDtypeStruct((8, 72, 128), F32),
            jax.ShapeDtypeStruct((8, 56, 128), F32),
            jax.ShapeDtypeStruct((320, 128), F32),
            jax.ShapeDtypeStruct((2, 128), F32),
        ),
        in_specs=[hbm] * 14,
        out_specs=(hbm,) * 4,
        scratch_shapes=[
            pltpu.SMEM((NLEV,), F32), pltpu.SMEM((NLEV,), F32),
            pltpu.SMEM((FIELDS,), F32), pltpu.SMEM((FIELDS,), F32),
            vmem(2, 128), vmem(2, 128, dtype=jnp.int32), vmem(2, 128, dtype=jnp.int32),
            vmem(4, 256, dtype=jnp.int32), vmem(4, 256),
            vmem(2, 1008, 128), vmem(2, DYN_STEPS, 13, QS, 40, 128), vmem(2, 4, 40, 128),
            *[vmem(8, 72, 128)] * 5, *[vmem(8, 56, 128)] * 5,
            vmem(LEV, 8, 128), vmem(LEV, 8, 128),
            vmem(320, 128),
            vmem(NBR, 1536, dtype=jnp.int32), vmem(NW, 1536, dtype=jnp.int32), vmem(NW, 1536),
            vmem(NT * OROW, 128), vmem(NT, PARTS * OROW, 128, dtype=BF16),
            vmem(NT - 2, 384, 128, dtype=BF16), vmem(NT * OROW, 128), vmem(16, 128),
            vmem(320, 128), vmem(2, 128),
            vmem(8, 128), vmem(8, 128), vmem(8, 128),
            dma((14,)), dma((2,)), dma((2,)), dma((8,)), dma((8,)),
            *[dma((2,))] * 6, dma((4,)),
            dma((2,)), dma((2,)), dma((2,)),
        ],
        compiler_params=pltpu.CompilerParams(
            collective_id=0, has_side_effects=True, vmem_limit_bytes=60 * 1024 * 1024
        ),
    )(
        atm, level_diffusion, level_wind, vertical_rate, convective_rate,
        ocean_skin.reshape(2, 128), trigger.reshape(2, 128), group_order.reshape(2, 128),
        ocean, ocean_neighbors, flux_sources, flux_weights, surface_sources, surface_weights,
    )
    new_atm, new_ocean, surf = pl.pallas_call(
        finish,
        out_shape=(
            jax.ShapeDtypeStruct((1008, 128), F32),
            jax.ShapeDtypeStruct((320, 128), F32),
            jax.ShapeDtypeStruct((2, 128), F32),
        ),
        in_specs=[hbm] * 4,
        out_specs=(hbm,) * 3,
        scratch_shapes=[
            vmem(8, 72, 128), vmem(8, 56, 128), vmem(320, 128), vmem(2, 128), vmem(1008, 128), dma((8,)),
        ],
        compiler_params=pltpu.CompilerParams(vmem_limit_bytes=60 * 1024 * 1024),
    )(*parts)
    new_atm = new_atm.reshape(FIELDS, NLEV, QS, ROWS, 128).transpose(0, 1, 3, 2, 4)
    new_ocean = new_ocean.reshape(OLEV, 8, 2, 128).transpose(0, 2, 1, 3).reshape(OLEV, 2, 1024)
    return (
        new_atm.reshape(FIELDS, NLEV, ROWS, QS * 128),
        new_ocean.transpose(1, 0, 2),
        surf.reshape(256),
    )


def solution(mesh):
    both = ("atm", "ocn")
    return jax.shard_map(
        functools.partial(local, mesh.shape["atm"], mesh.shape["ocn"]),
        mesh=mesh,
        in_specs=(
            P(None, "ocn", "atm", None), P("ocn"), P("ocn"), P(), P(),
            P(both), P(both), P(both), P(None, None, both),
            P(None, both), P(None, both), P(None, both), P(None, both), P(None, both),
        ),
        out_specs=(P(None, "ocn", "atm", None), P(None, None, both), P(both)),
        check_vma=False,
    )
```

```python
import functools

import jax
import jax.numpy as jnp
from jax import lax
from jax.experimental import pallas as pl
from jax.experimental.pallas import tpu as pltpu
from jax.sharding import PartitionSpec as P

MESH = pl.DeviceIdType.MESH
F32 = jnp.float32
BF16 = jnp.bfloat16

FIELDS = 7
LEV = 72
NLEV = 9
ROWS = 4
QS = 4
DYN_STEPS = 4
PHYS_ITERS = 3
CONV_ITERS = 24
OLEV = 20
OSTEPS = 4
NBR = 6
NW = 4
PARTS = 3
OROW = 48
NT = 12
OCEAN_SPREAD = 0.6
OCEAN_VERTICAL = 0.2
HEAT_COEF = 0.5
MOIST_COEF = 0.5
HEAT_BACK = 0.3
MOIST_BACK = 0.3
OCEAN_FORCE = 0.3

GROUPS = ((0, 4), (4, 3))
HSUB = 16


def iota(shape, dim):
    return lax.broadcasted_iota(jnp.int32, shape, dim)


def kernel(
    n_atm,
    n_ocn,
    atm, ld, lw, vr, cr, skin, trig, order, ocean, nbr, fsrc, fw, ssrc, sw,
    ba0, ba1, out_ocean, out_surf,
    ld_s, lw_s, vr_s, cr_s, skin_v, trig_v, order_v, ssrc_v, sw_v,
    nb, dd, coef,
    sa0, ra0, sc0, rc0, pa0, sa1, ra1, sc1, rc1, pa1,
    xa, xb,
    oc_o, nbr_e, fsrc_e, fw_e, el_out, er_out, el_in, er_in,
    st, hs, mm, ff, uu, oout, sout,
    fl, fl_l, fl_r,
    local_sem, halo_send, halo_recv, oh_send, oh_recv,
    a_send, a_recv, b_send, b_recv, c_send, c_recv, self_sem, f_send, f_recv, out_sem,
):
    a = lax.axis_index("atm")
    o = lax.axis_index("ocn")
    dev = a * n_ocn + o
    odd = lax.rem(a, 2)
    mate = a + 1 - 2 * odd
    cross = lax.rem(a + n_atm - 1 + 2 * odd, n_atm)
    total = n_atm * n_ocn
    left = lax.rem(dev + total - 1, total)
    right = lax.rem(dev + 1, total)
    left_id = (left // n_ocn, lax.rem(left, n_ocn))
    right_id = (right // n_ocn, lax.rem(right, n_ocn))
    def at_offset(dx, dy):
        return lax.rem(o // 2 + dx, n_ocn // 2) * 2 + lax.rem(o + dy, 2)

    peers = [at_offset(*d) for d in ((2, 1), (1, 1), (3, 1), (2, 0), (1, 0), (3, 0), (0, 1))]
    others = [at_offset(*d) for d in ((2, 0), (1, 0), (3, 0), (2, 1), (0, 0), (1, 1), (3, 1), (0, 1))]

    fills = [
        (ld, ld_s), (lw, lw_s), (vr, vr_s), (cr, cr_s),
        (skin, skin_v), (trig, trig_v), (order, order_v), (ssrc, ssrc_v), (sw, sw_v),
        (atm, nb.at[0]), (ocean, oc_o),
        (nbr, nbr_e.at[:, pl.ds(256, 1024)]),
        (fsrc, fsrc_e.at[:, pl.ds(256, 1024)]),
        (fw, fw_e.at[:, pl.ds(256, 1024)]),
    ]
    fills = [
        pltpu.make_async_copy(src, dst, local_sem.at[i]) for i, (src, dst) in enumerate(fills)
    ]
    for copy in fills:
        copy.start()

    edge_row = jnp.where(odd == 1, n_atm - 1, 0)
    inside = a != edge_row
    keep = jnp.where(inside, 1.0, 0.0).astype(F32)
    barrier = pltpu.get_barrier_semaphore()
    partners = [(mate, o), left_id, right_id] + [(a, p) for p in peers]

    def greet(devices):
        for device in devices:
            pl.semaphore_signal(barrier, inc=1, device_id=device, device_id_type=MESH)

    greet(partners)

    @pl.when(inside)
    def _():
        greet([(cross, p) for p in others])

    def remote(src, dst, send, recv, device):
        return pltpu.make_async_remote_copy(
            src_ref=src, dst_ref=dst, send_sem=send, recv_sem=recv,
            device_id=device, device_id_type=MESH,
        )

    for copy in fills:
        copy.wait()

    sends = (sa0, sa1)
    takes = (ra0, ra1)
    gives = (sc0, sc1)
    adds = (rc0, rc1)
    packs = (pa0, pa1)
    backs = (ba0, ba1)

    def enter(g, b):
        f0, nf = GROUPS[g]
        n = nf * NLEV
        for q in range(QS):
            block = [
                nb[b, pl.ds(f0 * NLEV * HSUB + 4 * q + r, n, stride=HSUB), :] for r in range(ROWS)
            ]
            for r in range(ROWS):
                piece = jnp.where(odd == 1, block[ROWS - 1 - r], block[r])
                dd[g, 0, 1 + (b + 1) * ROWS + r, q, pl.ds(0, n), :] = piece

    def update(g, step, i):
        n = GROUPS[g][1] * NLEV
        rows = pl.ds(0, n)
        lane = iota((n, 128), 1)
        here = [dd[g, step - 1, i, q, rows, :] for q in range(QS)]
        to_east = [pltpu.roll(x, 1, 1) for x in here]
        to_west = [pltpu.roll(x, 127, 1) for x in here]
        new = []
        for q in range(QS):
            west = jnp.where(lane == 0, to_east[(q - 1) % QS], to_east[q])
            east = jnp.where(lane == 127, to_west[(q + 1) % QS], to_west[q])
            beside = dd[g, step - 1, i - 1, q, rows, :] + dd[g, step - 1, i + 1, q, rows, :]
            new.append(
                coef[g, 0, rows, :] * here[q]
                + coef[g, 1, rows, :] * beside
                + coef[g, 2, rows, :] * east
                + coef[g, 3, rows, :] * west
            )
        return new

    def steps(g, first, dst):
        n = GROUPS[g][1] * NLEV

        def scaled(i, value):
            return value * jnp.where(i <= ROWS, keep, 1.0) if first <= ROWS else value

        for step in range(1, DYN_STEPS):

            def row(i, carry):
                for q, value in enumerate(update(g, step, i)):
                    dd[g, step, i, q, pl.ds(0, n), :] = scaled(i, value)
                return carry

            begin = first + DYN_STEPS - step
            lax.fori_loop(begin, begin + ROWS, row, 0, unroll=True)

        def last(i, carry):
            r = jnp.where(odd == 1, ROWS - 1 - i, i)
            for q, value in enumerate(update(g, DYN_STEPS, i + first)):
                dst[r * 2 + q // 2, pl.ds((q % 2) * n, n), :] = scaled(i + first, value)
            return carry

        lax.fori_loop(0, ROWS, last, 0, unroll=True)

    def contribute(g):
        n = GROUPS[g][1] * NLEV
        sub = lax.rem(iota((n, 128), 0), NLEV)
        diff = jnp.zeros((n, 128), F32)
        wind = jnp.zeros((n, 128), F32)
        for l in range(NLEV):
            diff = jnp.where(sub == l, ld_s[l], diff)
            wind = jnp.where(sub == l, lw_s[l], wind)
        coef[g, 0, pl.ds(0, n), :] = 1.0 - 4.0 * diff
        coef[g, 1, pl.ds(0, n), :] = diff
        coef[g, 2, pl.ds(0, n), :] = diff - 0.5 * wind
        coef[g, 3, pl.ds(0, n), :] = diff + 0.5 * wind
        none = jnp.zeros((n, 128), F32)
        for step in range(DYN_STEPS):
            for q in range(QS):
                for i in (ROWS - 1 - step, ROWS - step):
                    dd[g, step, i, q, pl.ds(0, n), :] = none
        enter(g, 0)
        steps(g, 1, gives[g])

    def send_across(g):
        copies = [
            remote(gives[g].at[p], adds[g].at[o], c_send.at[g], c_recv.at[g], (cross, p))
            for p in others
        ]
        whole = remote(gives[g], adds[g], c_send.at[g], c_recv.at[g], (cross, o))

        @pl.when(inside)
        def _():
            for copy in copies:
                copy.start()

        @pl.when(jnp.logical_not(inside))
        def _():
            adds[g][...] = jnp.zeros(adds[g].shape, F32)

        return whole

    contribute(0)

    @pl.when(inside)
    def _():
        pl.semaphore_wait(barrier, len(partners) + len(others))

    @pl.when(jnp.logical_not(inside))
    def _():
        pl.semaphore_wait(barrier, len(partners))

    halos = []
    for g, (f0, nf) in enumerate(GROUPS):
        rows = pl.ds(f0 * NLEV * HSUB, nf * NLEV * HSUB)
        copy = remote(atm.at[rows], nb.at[1, rows], halo_send.at[g], halo_recv.at[g], (mate, o))
        copy.start()
        halos.append(copy)

    unused = jnp.zeros((4, 128), F32)
    for u in range(2, 10):
        for f in range(2):
            piece = oc_o[pl.ds((u - 2) * 2 + f, OLEV, stride=16), :]
            st[pl.ds(u * OROW + f * 24, OLEV), :] = piece
            st[pl.ds(u * OROW + f * 24 + OLEV, 4), :] = unused

    sides = ((el_out, 8, 1152, el_in, right_id), (er_out, 2, 256, er_in, left_id))
    for buf, u, at, _, _ in sides:
        for k in range(4):
            buf[pl.ds(k * OLEV, OLEV), :] = st[pl.ds(u * OROW + k * 24, OLEV), :]
        buf[pl.ds(80, NBR), :] = nbr_e[:, pl.ds(at, 128)].astype(F32)
        buf[pl.ds(86, NW), :] = fsrc_e[:, pl.ds(at, 128)].astype(F32)
        buf[pl.ds(90, NW), :] = fw_e[:, pl.ds(at, 128)]
        buf[pl.ds(94, 2), :] = jnp.zeros((2, 128), F32)
    edges = [
        remote(buf, into, oh_send.at[i], oh_recv.at[i], device)
        for i, (buf, _, _, into, device) in enumerate(sides)
    ]
    for copy in edges:
        copy.start()

    out_cross = [send_across(0)]

    def exchange(src, dst, send, recv, own_sem, g):
        copies = [
            remote(src.at[p], dst.at[o], send.at[g], recv.at[g], (a, p)) for p in peers
        ]
        own = pltpu.make_async_copy(src.at[o], dst.at[o], own_sem)
        for copy in copies:
            copy.start()
        own.start()
        seven = pl.ds(0, n_ocn - 1)
        return remote(src.at[seven], dst.at[seven], send.at[g], recv.at[g], (a, peers[0])), own

    def crossed(handle):
        @pl.when(inside)
        def _():
            handle.wait_recv()

    def landed(handle):
        whole, own = handle
        own.wait()
        whole.wait_recv()

    out_there = []
    for g in range(2):
        halos[g].wait_recv()
        enter(g, 1)
        steps(g, 1 + ROWS, sends[g])
        out_there.append(exchange(sends[g], takes[g], a_send, a_recv, self_sem.at[g], g))
        if g == 0:
            contribute(1)
            out_cross.append(send_across(1))

    hit = jnp.where(trig_v[...] > 0, order_v[...], -1).astype(F32)
    hit = jnp.concatenate([hit, jnp.full((6, 128), -1.0, F32)], axis=0)
    hit = jnp.transpose(hit, (1, 0))
    lane = iota((128, 128), 1)
    active = []
    for half in range(2):
        column = (lane + 128 * half).astype(F32)
        mark = jnp.where(hit[:, 0:1] == column, 1.0, 0.0) + jnp.where(hit[:, 1:2] == column, 1.0, 0.0)
        active.append(jnp.sum(mark, axis=0, keepdims=True))

    for copy in edges:
        copy.wait()
    for buf, u, at in ((el_in, 0, 128), (er_in, 10, 1280)):
        for k in range(4):
            st[pl.ds(u * OROW + k * 24, OLEV), :] = buf[pl.ds(k * OLEV, OLEV), :]
            st[pl.ds(u * OROW + k * 24 + OLEV, 4), :] = unused
        nbr_e[:, pl.ds(at, 128)] = buf[pl.ds(80, NBR), :].astype(jnp.int32)
        fsrc_e[:, pl.ds(at, 128)] = buf[pl.ds(86, NW), :].astype(jnp.int32)
        fw_e[:, pl.ds(at, 128)] = buf[pl.ds(90, NW), :]

    def build(u, carry):
        at = pl.multiple_of(u * 128, 128)
        k = iota((192, 128), 0) + 96
        base = iota((1, 128), 1) + 128
        count = jnp.zeros((192, 128), F32)
        for j in range(NBR):
            target = nbr_e[pl.ds(j, 1), pl.ds(at, 128)] + base
            count = count + jnp.where(k == target, 1.0, 0.0)
        mm[u - 1, pl.ds(0, 96), :] = jnp.zeros((96, 128), BF16)
        mm[u - 1, pl.ds(96, 192), :] = count.astype(BF16)
        mm[u - 1, pl.ds(288, 96), :] = jnp.zeros((96, 128), BF16)
        return carry

    lax.fori_loop(1, NT - 1, build, 0, unroll=True)

    level_row = lax.rem(iota((OROW, 128), 0), 24)

    def spread(force):
        def split(u, carry):
            rest = st[pl.ds(pl.multiple_of(u * OROW, OROW), OROW), :]
            for part in range(PARTS):
                piece = rest.astype(BF16)
                hs[u, pl.ds(part * OROW, OROW), :] = piece
                rest = rest - piece.astype(F32)
            return carry

        lax.fori_loop(0, NT, split, 0, unroll=True)

        def tile(u, carry):
            source = jnp.concatenate([hs[u - 1], hs[u], hs[u + 1]], axis=1)
            sums = jnp.dot(source, mm[u - 1], preferred_element_type=F32)
            around = sums[0:OROW]
            for part in range(1, PARTS):
                around = around + sums[part * OROW : (part + 1) * OROW]
            rows = pl.ds(pl.multiple_of(u * OROW, OROW), OROW)
            here = st[rows, :]
            here = here + OCEAN_SPREAD * (around * (1.0 / 6.0) - here)
            above = jnp.where(level_row == 0, here, pltpu.roll(here, 1, 0))
            below = jnp.where(level_row == OLEV - 1, here, pltpu.roll(here, OROW - 1, 0))
            here = here + OCEAN_VERTICAL * (above + below - 2.0 * here)
            if force:
                here = here + ff[pl.ds(pl.multiple_of(u * OROW, OROW), OROW), :]
            st[rows, :] = jnp.where(level_row < OLEV, here, 0.0)
            return carry

        lax.fori_loop(1, NT - 1, tile, 0, unroll=True)

    spread(False)

    def physics(g):
        f0, nf = GROUPS[g]
        n = 2 * nf
        x = (xa, xb)[g]
        sub = iota((n, 128), 0)
        field = lax.rem(sub, nf)
        mix = jnp.zeros((n, 128), F32)
        rate = jnp.zeros((n, 128), F32)
        for f in range(nf):
            mix = jnp.where(field == f, vr_s[f0 + f], mix)
            rate = jnp.where(field == f, cr_s[f0 + f], rate)
        rate = rate * jnp.where(sub < nf, active[0], active[1])

        for lev in range(LEV):
            rows = pl.ds(lev % NLEV, n, stride=NLEV)
            x[lev, pl.ds(0, n), :] = takes[g][lev // NLEV, rows, :] + adds[g][lev // NLEV, rows, :]

        def vertical(i, carry):
            here = x[0, pl.ds(0, n), :]
            above = here
            for lev in range(LEV):
                below = x[lev + 1, pl.ds(0, n), :] if lev < LEV - 1 else here
                x[lev, pl.ds(0, n), :] = here + mix * (above + below - 2.0 * here)
                above, here = here, below
            return carry

        lax.fori_loop(0, PHYS_ITERS, vertical, 0)

        def convect(i, carry):
            here = x[0, pl.ds(0, n), :]
            came = jnp.zeros((n, 128), F32)
            for lev in range(LEV - 1):
                below = x[lev + 1, pl.ds(0, n), :]
                transfer = rate * jnp.tanh(below - here)
                x[lev, pl.ds(0, n), :] = here + transfer - came
                came, here = transfer, below
            x[LEV - 1, pl.ds(0, n), :] = here - came
            return carry

        lax.fori_loop(0, CONV_ITERS, convect, 0)

    def pack(g):
        nf = GROUPS[g][1]
        n = 2 * nf
        x = (xa, xb)[g]
        for lev in range(LEV):
            packs[g][lev // NLEV, pl.ds(lev % NLEV, n, stride=NLEV), :] = x[lev, pl.ds(0, n), :]

    landed(out_there[0])
    crossed(out_cross[0])
    physics(0)

    fl[...] = jnp.zeros((8, 128), F32)
    for half in range(2):
        low_row = [xa[LEV - 1, pl.ds(half * 4 + f, 1), :] for f in range(4)]
        speed = jnp.sqrt(1.0 + low_row[1] * low_row[1] + low_row[2] * low_row[2])
        heat = HEAT_COEF * speed * (low_row[0] - skin_v[pl.ds(half, 1), :])
        fresh = MOIST_COEF * speed * low_row[3]
        xa[LEV - 1, pl.ds(half * 4, 1), :] = low_row[0] - HEAT_BACK * heat
        xa[LEV - 1, pl.ds(half * 4 + 3, 1), :] = low_row[3] - MOIST_BACK * fresh
        fl[pl.ds(2 * half, 1), :] = heat
        fl[pl.ds(2 * half + 1, 1), :] = fresh
    fluxes = [
        remote(fl, fl_l, f_send.at[0], f_recv.at[0], right_id),
        remote(fl, fl_r, f_send.at[1], f_recv.at[1], left_id),
    ]
    for copy in fluxes:
        copy.start()
    pack(0)
    back_home = [exchange(packs[0], backs[0], b_send, b_recv, self_sem.at[2], 0)]
    landed(out_there[1])
    crossed(out_cross[1])
    physics(1)
    pack(1)
    back_home.append(exchange(packs[1], backs[1], b_send, b_recv, self_sem.at[3], 1))

    for copy in fluxes:
        copy.wait_recv()
    near = jnp.concatenate(
        [
            fl_l[pl.ds(2, 1), :], fl[pl.ds(0, 1), :], fl[pl.ds(2, 1), :], fl_r[pl.ds(0, 1), :],
            fl_l[pl.ds(3, 1), :], fl[pl.ds(1, 1), :], fl[pl.ds(3, 1), :], fl_r[pl.ds(1, 1), :],
        ],
        axis=0,
    )
    sub8 = iota((8, 128), 0)
    chunk = lax.rem(sub8, 4)
    ff[...] = jnp.zeros(ff.shape, F32)
    for u in range(1, NT - 1):
        at = pl.ds(u * 128, 128)
        acc = jnp.zeros((8, 128), F32)
        for link in range(NW):
            source = fsrc_e[pl.ds(link, 1), at] - (dev * 256 - 128)
            source = jnp.broadcast_to(source, (8, 128))
            picked = jnp.take_along_axis(near, source & 127, axis=1, mode="promise_in_bounds")
            picked = jnp.where((source >> 7) == chunk, picked, 0.0)
            acc = acc + fw_e[pl.ds(link, 1), at] * picked
        ff[pl.ds(u * OROW, 1), :] = OCEAN_FORCE * jnp.sum(acc[0:4], axis=0, keepdims=True)
        ff[pl.ds(u * OROW + 24, 1), :] = OCEAN_FORCE * jnp.sum(acc[4:8], axis=0, keepdims=True)
    for u in range(1, NT - 1):
        for f in range(2):
            row = pl.ds(u * OROW + 24 * f, 1)
            st[row, :] = st[row, :] + ff[row, :]

    def ocean_step(i, carry):
        spread(True)
        return carry

    lax.fori_loop(1, OSTEPS, ocean_step, 0)

    for u in range(2, 10):
        for f in range(2):
            oout[pl.ds((u - 2) * 2 + f, OLEV, stride=16), :] = st[pl.ds(u * OROW + f * 24, OLEV), :]
    ocean_copy = pltpu.make_async_copy(oout, out_ocean, out_sem.at[0])
    ocean_copy.start()

    uu[...] = jnp.zeros(uu.shape, F32)
    for u in range(1, NT - 1):
        uu[pl.ds(u, 1), :] = st[pl.ds(u * OROW, 1), :]
    top = (uu[pl.ds(0, 8), :], uu[pl.ds(8, 8), :])
    for half in range(2):
        at = pl.ds(half * 128, 128)
        acc = jnp.zeros((8, 128), F32)
        for link in range(NW):
            source = ssrc_v[pl.ds(link, 1), at] - (dev * 1024 - 256)
            source = jnp.broadcast_to(source, (8, 128))
            weight = sw_v[pl.ds(link, 1), at]
            for part in range(2):
                picked = jnp.take_along_axis(top[part], source & 127, axis=1, mode="promise_in_bounds")
                picked = jnp.where((source >> 7) == sub8 + 8 * part, picked, 0.0)
                acc = acc + weight * picked
        sout[pl.ds(half, 1), :] = jnp.sum(acc, axis=0, keepdims=True)
    surf_copy = pltpu.make_async_copy(sout, out_surf, out_sem.at[1])
    surf_copy.start()

    for copy in halos + fluxes:
        copy.wait_send()
    for whole, own in out_there:
        whole.wait_send()

    @pl.when(inside)
    def _():
        for whole in out_cross:
            whole.wait_send()

    for whole, own in back_home:
        whole.wait_send()
    for handle in back_home:
        landed(handle)
    ocean_copy.wait()
    surf_copy.wait()


def finish(ba0, ba1, ocean, surf, out_atm, out_ocean, out_surf, b0, b1, ocean_v, surf_v, out_v, sem):
    ins = ((ba0, b0), (ba1, b1), (ocean, ocean_v), (surf, surf_v))
    copies = [pltpu.make_async_copy(src, dst, sem.at[i]) for i, (src, dst) in enumerate(ins)]
    for copy in copies:
        copy.start()
    outs = []
    for g, (f0, nf) in enumerate(GROUPS):
        n = nf * NLEV
        copies[g].wait()
        for r in range(ROWS):
            for q in range(QS):
                piece = (b0, b1)[g][2 * r + q // 2, pl.ds((q % 2) * n, n), :]
                out_v[pl.ds(f0 * NLEV * HSUB + 4 * q + r, n, stride=HSUB), :] = piece
        rows = pl.ds(f0 * NLEV * HSUB, n * HSUB)
        outs.append(pltpu.make_async_copy(out_v.at[rows], out_atm.at[rows], sem.at[4 + g]))
        outs[-1].start()
    for i, (src, dst) in enumerate(((ocean_v, out_ocean), (surf_v, out_surf))):
        copies[2 + i].wait()
        outs.append(pltpu.make_async_copy(src, dst, sem.at[6 + i]))
        outs[-1].start()
    for copy in outs:
        copy.wait()


def local(n_atm, n_ocn, atm_state, level_diffusion, level_wind, vertical_rate, convective_rate,
          ocean_skin, trigger, group_order, ocean_state, ocean_neighbors, flux_sources,
          flux_weights, surface_sources, surface_weights):
    atm = atm_state.reshape(FIELDS, NLEV, ROWS, QS, 128).transpose(0, 1, 3, 2, 4).reshape(1008, 128)
    ocean = ocean_state.transpose(1, 0, 2).reshape(OLEV, 2, 8, 128).transpose(0, 2, 1, 3).reshape(320, 128)
    hbm = pl.BlockSpec(memory_space=pltpu.HBM)
    dma = pltpu.SemaphoreType.DMA

    def vmem(*shape, dtype=F32):
        return pltpu.VMEM(shape, dtype)

    parts = pl.pallas_call(
        functools.partial(kernel, n_atm, n_ocn),
        out_shape=(
            jax.ShapeDtypeStruct((8, 72, 128), F32),
            jax.ShapeDtypeStruct((8, 56, 128), F32),
            jax.ShapeDtypeStruct((320, 128), F32),
            jax.ShapeDtypeStruct((2, 128), F32),
        ),
        in_specs=[hbm] * 14,
        out_specs=(hbm,) * 4,
        scratch_shapes=[
            pltpu.SMEM((NLEV,), F32), pltpu.SMEM((NLEV,), F32),
            pltpu.SMEM((FIELDS,), F32), pltpu.SMEM((FIELDS,), F32),
            vmem(2, 128), vmem(2, 128, dtype=jnp.int32), vmem(2, 128, dtype=jnp.int32),
            vmem(4, 256, dtype=jnp.int32), vmem(4, 256),
            vmem(2, 1008, 128), vmem(2, DYN_STEPS, 13, QS, 40, 128), vmem(2, 4, 40, 128),
            *[vmem(8, 72, 128)] * 5, *[vmem(8, 56, 128)] * 5,
            vmem(LEV, 8, 128), vmem(LEV, 8, 128),
            vmem(320, 128),
            vmem(NBR, 1536, dtype=jnp.int32), vmem(NW, 1536, dtype=jnp.int32), vmem(NW, 1536),
            *[vmem(96, 128)] * 4,
            vmem(NT * OROW, 128), vmem(NT, PARTS * OROW, 128, dtype=BF16),
            vmem(NT - 2, 384, 128, dtype=BF16), vmem(NT * OROW, 128), vmem(16, 128),
            vmem(320, 128), vmem(2, 128),
            vmem(8, 128), vmem(8, 128), vmem(8, 128),
            dma((14,)), dma((2,)), dma((2,)), dma((8,)), dma((8,)),
            *[dma((2,))] * 6, dma((4,)),
            dma((2,)), dma((2,)), dma((2,)),
        ],
        compiler_params=pltpu.CompilerParams(
            collective_id=0, has_side_effects=True, vmem_limit_bytes=60 * 1024 * 1024
        ),
    )(
        atm, level_diffusion, level_wind, vertical_rate, convective_rate,
        ocean_skin.reshape(2, 128), trigger.reshape(2, 128), group_order.reshape(2, 128),
        ocean, ocean_neighbors, flux_sources, flux_weights, surface_sources, surface_weights,
    )
    new_atm, new_ocean, surf = pl.pallas_call(
        finish,
        out_shape=(
            jax.ShapeDtypeStruct((1008, 128), F32),
            jax.ShapeDtypeStruct((320, 128), F32),
            jax.ShapeDtypeStruct((2, 128), F32),
        ),
        in_specs=[hbm] * 4,
        out_specs=(hbm,) * 3,
        scratch_shapes=[
            vmem(8, 72, 128), vmem(8, 56, 128), vmem(320, 128), vmem(2, 128), vmem(1008, 128), dma((8,)),
        ],
        compiler_params=pltpu.CompilerParams(vmem_limit_bytes=60 * 1024 * 1024),
    )(*parts)
    new_atm = new_atm.reshape(FIELDS, NLEV, QS, ROWS, 128).transpose(0, 1, 3, 2, 4)
    new_ocean = new_ocean.reshape(OLEV, 8, 2, 128).transpose(0, 2, 1, 3).reshape(OLEV, 2, 1024)
    return (
        new_atm.reshape(FIELDS, NLEV, ROWS, QS * 128),
        new_ocean.transpose(1, 0, 2),
        surf.reshape(256),
    )


def solution(mesh):
    both = ("atm", "ocn")
    return jax.shard_map(
        functools.partial(local, mesh.shape["atm"], mesh.shape["ocn"]),
        mesh=mesh,
        in_specs=(
            P(None, "ocn", "atm", None), P("ocn"), P("ocn"), P(), P(),
            P(both), P(both), P(both), P(None, None, both),
            P(None, both), P(None, both), P(None, both), P(None, both), P(None, both),
        ),
        out_specs=(P(None, "ocn", "atm", None), P(None, None, both), P(both)),
        check_vma=False,
    )
```
